512 devices in a mesh: clip: 8 (over y, x_hi), tok: 64 (over x_lo, z, core).
Axes of the slice: x: 4 (x_hi: 2, x_lo: 2; x = x_hi * 2 + x_lo), y: 4, z: 16, core: 2. Of those that a mesh axis runs over, the one named last changes fastest.
Arguments:
- student_hidden: bfloat16 [8, 16384, 1024], P('clip', 'tok'), may hold values from -120 to 120
- teacher_tokens: bfloat16 [8, 16384, 1024], P('clip', 'tok'), may hold values from -120 to 120
- proj_weight: bfloat16 [1024, 1024], replicated, may hold values from -0.1875 to 0.1875
Outputs:
- hidden_grad: bfloat16 [8, 16384, 1024], P('clip', 'tok')
- weight_grad: float32 [1024, 1024], P('tok')
The draws below stay inside these ranges and needn't reach their ends.
All inputs are finite; a program needn't handle non-finite values.
Results may differ from the reference program's by a relative error of at most 0.012.
Values may be sent and summed in bfloat16 or wider, within the bound.
A program may use at most 64 MiB of HBM per device.

```python
import math
import jax
import jax.numpy as jnp
from jax import lax

FEAT = 1024
HID = 1024
TOK_DEV = 256
BAND = 4
TOKENS = 16384
CLIPS = 8
N_TOK = 64


def draw_student_hidden(key, part):
    key = jax.random.fold_in(key, 11)
    subkeys = jax.random.split(key, 3)
    shape = (CLIPS, TOKENS, HID)
    row_scale = jnp.exp(jax.random.uniform(subkeys[0], (CLIPS, TOKENS, 1), jnp.float32, 0.0, math.log(10.0)))
    col_scale = jnp.exp(jax.random.uniform(subkeys[1], (1, 1, HID), jnp.float32, math.log(0.3), math.log(3.0)))
    values = jnp.clip(jax.random.normal(subkeys[2], shape, jnp.float32), -4.0, 4.0)
    return (values * row_scale * col_scale).astype(jnp.bfloat16)


def draw_teacher_tokens(key, part):
    key = jax.random.fold_in(key, 23)
    subkeys = jax.random.split(key, 3)
    shape = (CLIPS, TOKENS, FEAT)
    row_scale = jnp.exp(jax.random.uniform(subkeys[0], (CLIPS, TOKENS, 1), jnp.float32, 0.0, math.log(10.0)))
    col_scale = jnp.exp(jax.random.uniform(subkeys[1], (1, 1, FEAT), jnp.float32, math.log(0.3), math.log(3.0)))
    values = jnp.clip(jax.random.normal(subkeys[2], shape, jnp.float32), -4.0, 4.0)
    return (values * row_scale * col_scale).astype(jnp.bfloat16)


def gaussian(rng, extent, deviation, limit, kind=jnp.bfloat16):
    return jnp.clip(deviation * jax.random.normal(rng, extent, jnp.float32), -limit, limit).astype(kind)


def setup_inputs(seed: int = 0) -> dict:
    seeds = jax.random.split(jax.random.key(seed), 4)
    student_hidden = draw_student_hidden(jax.random.fold_in(seeds[3], 71), 0)
    teacher_tokens = draw_teacher_tokens(jax.random.fold_in(seeds[3], 71), 0)
    proj_weight = gaussian(seeds[2], (HID, FEAT), HID ** -0.5, 0.1875)
    return dict(student_hidden=student_hidden, teacher_tokens=teacher_tokens, proj_weight=proj_weight)


EPSILON = 1e-06

def unit_rows(values):
    row_norm = jnp.sqrt(lax.optimization_barrier(jnp.sum(values * values, axis=-1, keepdims=True)) + EPSILON)
    return (values / row_norm, row_norm)

def later_blocks(values, distance):
    padding = jnp.zeros(values.shape[:1] + (distance,) + values.shape[2:], values.dtype)
    return jnp.concatenate([values[:, distance:], padding], axis=1)

def earlier_blocks(values, distance):
    padding = jnp.zeros(values.shape[:1] + (distance,) + values.shape[2:], values.dtype)
    return jnp.concatenate([padding, values[:, :-distance]], axis=1)

def relation(first_s, second_s, first_t, second_t):
    return jnp.einsum('cbif,cbjf->cbij', first_s, second_s) - jnp.einsum('cbif,cbjf->cbij', first_t, second_t)

def reference(student_hidden, teacher_tokens, proj_weight):
    hidden32 = student_hidden.astype(jnp.float32).reshape(CLIPS, N_TOK, TOK_DEV, HID)
    weight32 = proj_weight.astype(jnp.float32)
    projected = jnp.einsum('cbth,hf->cbtf', hidden32, weight32)
    unit, row_norm = unit_rows(projected)
    student_unit = lax.optimization_barrier(unit.astype(jnp.bfloat16)).astype(jnp.float32)
    teacher32 = teacher_tokens.astype(jnp.float32).reshape(CLIPS, N_TOK, TOK_DEV, FEAT)
    teacher_unit = lax.optimization_barrier(unit_rows(teacher32)[0].astype(jnp.bfloat16)).astype(jnp.float32)
    own_diff = relation(student_unit, student_unit, teacher_unit, teacher_unit)
    own_weight = 128.0 * (own_diff + jnp.swapaxes(own_diff, 2, 3))
    own_weight = lax.optimization_barrier(own_weight.astype(jnp.bfloat16)).astype(jnp.float32)
    unit_grad = jnp.einsum('cbij,cbjf->cbif', own_weight, student_unit)
    for distance in range(1, BAND + 1):
        far_student = later_blocks(student_unit, distance)
        far_teacher = later_blocks(teacher_unit, distance)
        pair_diff = relation(student_unit, far_student, teacher_unit, far_teacher)
        pair_weight = lax.optimization_barrier((256.0 * pair_diff).astype(jnp.bfloat16)).astype(jnp.float32)
        unit_grad = unit_grad + jnp.einsum('cbij,cbjf->cbif', pair_weight, far_student)
        returned = jnp.einsum('cbij,cbif->cbjf', pair_weight, student_unit)
        unit_grad = unit_grad + earlier_blocks(returned, distance)
    along = lax.optimization_barrier(jnp.sum(unit * unit_grad, axis=-1, keepdims=True))
    proj_grad = ((unit_grad - unit * along) / row_norm).astype(jnp.bfloat16)
    proj_grad32 = lax.optimization_barrier(proj_grad).astype(jnp.float32)
    hidden_grad = jnp.einsum('cbtf,hf->cbth', proj_grad32, weight32).astype(jnp.bfloat16)
    weight_grad = jnp.einsum('cbth,cbtf->hf', hidden32, proj_grad32) / (4.0 * TOK_DEV)
    return (hidden_grad.reshape(CLIPS, TOKENS, HID), weight_grad)
```

```python
import jax
import jax.numpy as jnp
from jax import lax
from jax.experimental import pallas as pl
from jax.experimental.pallas import tpu as pltpu
from jax.sharding import PartitionSpec as P

EPSILON = 1e-06
MESH = pl.DeviceIdType.MESH
BF16 = jnp.bfloat16
F32 = jnp.float32
ROWS = 256
FEAT = 1024
NZ, NY, NX, NCLIP = 16, 4, 4, 8
CHAINS = 32
HALF = 2
STEP = 32


def dot_nn(a, b):
    return jnp.dot(a, b, preferred_element_type=F32)


def dot_nt(a, b):
    return lax.dot_general(a, b, (((1,), (1,)), ((), ())), preferred_element_type=F32)


def kernel(
    h_ref, t_ref, w_ref, hg_ref, wg_ref,
    wv, hr, tr, su, tu, proj, inv, dt, e_near, e_far, g, pall, ht,
    ws, wr, a0, a1, r0, r1, b0, b1, s0, s1, zs, zr, ag, pf, hgv, ov,
    load_sem, store_sem, halo_s, halo_r, fwd_s, fwd_r, pf_s, pf_r,
    d2d_s, d2d_r, st1_s, st1_r, st1b_s, st1b_r, st2_s, st2_r, z_s, z_r, ag_s, ag_r,
):
    k = lax.axis_index("clip")
    b = lax.axis_index("tok")
    c = lax.rem(b, 2)
    q = b // 2
    z = lax.rem(q, NZ)
    xl = q // NZ
    y = k // 2
    xh = lax.rem(k, 2)
    x = xh * 2 + xl
    has = (q > 0, q < CHAINS - 1)

    def at(yy, xx, zz, cc):
        return {"clip": yy * 2 + xx // 2, "tok": lax.rem(xx, 2) * 32 + zz * 2 + cc}

    sib = {"clip": k, "tok": b + 1 - 2 * c}
    side = ({"clip": k, "tok": b - 2}, {"clip": k, "tok": b + 2})

    def y_peer(d):
        return at(lax.rem(y + d, NY), x, z, c)

    def x_peer(d):
        return at(y, lax.rem(x + d, NX), z, c)

    def z_peer(d):
        return at(y, x, lax.rem(z + d, NZ), c)

    def clip_peer(d):
        return {"clip": lax.rem(k + d, NCLIP), "tok": b}

    def remote(src, dst, ssem, rsem, dev):
        return pltpu.make_async_remote_copy(
            src_ref=src, dst_ref=dst, send_sem=ssem, recv_sem=rsem, device_id=dev, device_id_type=MESH
        )

    loads = [
        pltpu.make_async_copy(t_ref, tr.at[1], load_sem.at[0]),
        pltpu.make_async_copy(h_ref, hr.at[1], load_sem.at[1]),
        pltpu.make_async_copy(w_ref, wv, load_sem.at[2]),
    ]
    for cp in loads:
        cp.start()
    barrier = pltpu.get_barrier_semaphore()

    def greet(dev):
        pl.semaphore_signal(barrier, inc=1, device_id=dev, device_id_type=MESH)

    greet(sib)
    for i in range(2):
        @pl.when(has[i])
        def _(i=i):
            greet(side[i])
    greet(x_peer(1))
    greet(x_peer(3))
    for d in range(1, NCLIP):
        greet(clip_peer(d))
    for d in range(1, NZ):
        greet(z_peer(d))
    ends = jnp.where(q > 0, 1, 0) + jnp.where(q < CHAINS - 1, 1, 0)
    pl.semaphore_wait(barrier, 3 + (NCLIP - 1) + (NZ - 1) + ends)
    for cp in loads[:2]:
        cp.wait()

    hrows = ROWS // HALF

    def halo_copies(i):
        dst_slot = 2 - 2 * i
        copies = [remote(tr.at[1], tr.at[dst_slot], halo_s.at[i, 0], halo_r.at[i, 0], side[i])]
        for j in range(HALF):
            rows = pl.ds(j * hrows, hrows)
            copies.append(
                remote(
                    hr.at[1, rows], hr.at[dst_slot, rows], halo_s.at[i, 1 + j], halo_r.at[i, 1 + j], side[i]
                )
            )
        return copies

    halo = [halo_copies(0), halo_copies(1)]
    for n in range(1 + HALF):
        for i in range(2):
            @pl.when(has[i])
            def _(i=i, n=n):
                halo[i][n].start()

    def halo_arrival(slot, n):
        i = 0 if slot == 0 else 1
        src = halo[1 - i][n]

        @pl.when(has[i])
        def _():
            src.wait_recv()

        @pl.when(jnp.logical_not(has[i]))
        def _():
            if n == 0:
                tr[slot] = jnp.zeros((ROWS, FEAT), BF16)
            else:
                hr[slot, (n - 1) * hrows : n * hrows] = jnp.zeros((hrows, FEAT), BF16)

    def teacher_unit(slot):
        def body(i, carry):
            rows = pl.ds(pl.multiple_of(i * STEP, STEP), STEP)
            v = tr[slot, rows].astype(F32)
            r = lax.rsqrt(jnp.sum(v * v, axis=-1, keepdims=True) + EPSILON)
            tu[slot, 0, rows] = (v * r).astype(BF16)
            return carry

        lax.fori_loop(0, ROWS // STEP, body, 0)

    def student_unit(slot, r0_, n):
        rows_all = slice(r0_, r0_ + n)
        for nb in range(4):
            cols = slice(nb * 256, (nb + 1) * 256)
            proj[slot, rows_all, cols] = dot_nn(hr[slot, rows_all], wv[:, cols])

        def body(i, carry):
            rows = pl.ds(pl.multiple_of(r0_ + i * STEP, STEP), STEP)
            v = proj[slot, rows]
            r = lax.rsqrt(jnp.sum(v * v, axis=-1, keepdims=True) + EPSILON)
            inv[slot, rows] = jnp.broadcast_to(r, (STEP, 128))
            su[slot, 0, rows] = (v * r).astype(BF16)
            return carry

        lax.fori_loop(0, n // STEP, body, 0)

    def transposed(slot):
        for j in range(4):
            cols = slice(j * 256, (j + 1) * 256)
            v = hr[slot, :, cols].astype(F32).T.reshape(8, 2, 16, ROWS)
            for cc in range(2):
                ht[cc, j * 128 : (j + 1) * 128, slot * 256 : (slot + 1) * 256] = (
                    v[:, cc].reshape(128, ROWS).astype(BF16)
                )

    def forward(buf, slot, n):
        cp = remote(buf.at[slot, 0], buf.at[slot, 1], fwd_s.at[n, slot], fwd_r.at[n, slot], sib)
        cp.start()
        return cp

    fwd = {}
    teacher_unit(1)
    fwd["t1"] = forward(tu, 1, 0)
    loads[2].wait()
    student_unit(1, 0, ROWS)
    fwd["s1"] = forward(su, 1, 1)
    transposed(1)
    for slot in (0, 2):
        halo_arrival(slot, 0)
        teacher_unit(slot)
        fwd["t%d" % slot] = forward(tu, slot, 0)
    for slot in (1, 0, 2):
        fwd["t%d" % slot].wait_recv()

    def near_t(j, carry):
        dt[j] = dot_nt(tu[1, 0], tu[j // 2, lax.rem(j, 2)])
        return carry

    lax.fori_loop(0, 6, near_t, 0)
    for f in range(2):
        for who in range(2):
            dt[6 + f * 2 + who] = dot_nt(tu[2 * f, 0], tu[2 - 2 * f, who])

    for n in range(HALF):
        for slot in (0, 2):
            halo_arrival(slot, 1 + n)
            student_unit(slot, n * hrows, hrows)
            if n == HALF - 1:
                fwd["s%d" % slot] = forward(su, slot, 1)
    for slot in (0, 2):
        transposed(slot)
    for slot in (1, 0, 2):
        fwd["s%d" % slot].wait_recv()

    for j in range(6):
        e_near[:, j * 256 : (j + 1) * 256] = (
            256.0 * (dot_nt(su[1, 0], su[j // 2, j % 2]) - dt[j])
        ).astype(BF16)
    cross = (jnp.where(c == 1, 256.0, 0.0), jnp.where(c == 0, 256.0, 0.0))
    for f in range(2):
        for who in range(2):
            scale = 256.0 if who == 0 else cross[f]
            e_far[f, :, who * 256 : (who + 1) * 256] = (
                scale * (dot_nt(su[2 * f, 0], su[2 - 2 * f, who]) - dt[6 + f * 2 + who])
            ).astype(BF16)

    def stacked(lo, n, cols):
        return jnp.concatenate([su[(lo + i) // 2, (lo + i) % 2, :, cols] for i in range(n)], axis=0)

    for nb in range(4):
        cols = slice(nb * 256, (nb + 1) * 256)
        g[1, :, cols] = dot_nn(e_near[...], stacked(0, 6, cols))
        g[0, :, cols] = dot_nn(e_far[0], stacked(4, 2, cols))
        g[2, :, cols] = dot_nn(e_far[1], stacked(0, 2, cols))

    def project(slot):
        def body(i, carry):
            rows = pl.ds(pl.multiple_of(i * STEP, STEP), STEP)
            r = inv[slot, rows][:, :1]
            u = proj[slot, rows] * r
            v = g[slot, rows]
            along = jnp.sum(u * v, axis=-1, keepdims=True)
            out = pl.ds(pl.multiple_of(slot * ROWS + i * STEP, STEP), STEP)
            pall[out] = ((v - u * along) * r).astype(BF16)
            return carry

        lax.fori_loop(0, ROWS // STEP, body, 0)

    back = []
    for i, slot in ((0, 0), (1, 2)):
        project(slot)
        cp = remote(pall.at[pl.ds(slot * ROWS, ROWS)], pf.at[1 - i], pf_s.at[i], pf_r.at[i], side[i])
        back.append(cp)

        @pl.when(has[i])
        def _(cp=cp):
            cp.start()
    project(1)

    d2d = []
    for d in range(4):
        yy = lax.rem(y + 1 + d, NY)
        part = dot_nn(ht[1 - c], pall[:, pl.ds(pl.multiple_of(yy * 256, 256), 256)])
        for i in range(2):
            ws[d, i] = part[:, i * 128 : (i + 1) * 128].astype(BF16)
        cp = remote(ws.at[d], wr.at[d], d2d_s.at[d], d2d_r.at[d], sib)
        cp.start()
        d2d.append(cp)
    st1, st1b = [], []
    for d in range(4):
        dy = (1 + d) % 4
        yy = lax.rem(y + dy, NY)
        part = dot_nn(ht[c], pall[:, pl.ds(pl.multiple_of(yy * 256, 256), 256)])
        d2d[d].wait_recv()
        for i in range(2):
            v = (part[:, i * 128 : (i + 1) * 128] + wr[d, i].astype(F32)).astype(BF16)
            for j in range(2):
                a0[yy, i * 2 + j] = v[j * 256 : j * 256 + 128]
                a1[i * 2 + j, yy] = v[j * 256 + 128 : j * 256 + 256]
        if dy:
            cp = remote(a0.at[yy], r0.at[dy - 1], st1_s.at[dy - 1], st1_r.at[dy - 1], y_peer(dy))
            cp.start()
            st1.append(cp)
        for dx in range(1, NX):
            xx = lax.rem(x + dx, NX)
            cp = remote(
                a1.at[xx, yy], r1.at[dx - 1, yy], st1b_s.at[dx - 1, dy], st1b_r.at[dx - 1, dy], x_peer(dx)
            )
            cp.start()
            st1b.append(cp)

    st2 = []
    for cp in st1:
        cp.wait_recv()
    for dx in (1, 2, 3, 0):
        xx = lax.rem(x + dx, NX)
        v = a0[y, xx].astype(F32)
        for i in range(3):
            v = v + r0[i, xx].astype(F32)
        b0[xx] = v.astype(BF16)
        if dx:
            cp = remote(b0.at[xx], s0.at[dx - 1], st2_s.at[0, dx - 1], st2_r.at[0, dx - 1], x_peer(dx))
            cp.start()
            st2.append(cp)
    for cp in st1b:
        cp.wait_recv()
    for dy in (1, 2, 3, 0):
        yy = lax.rem(y + dy, NY)
        v = a1[x, yy].astype(F32)
        for i in range(3):
            v = v + r1[i, yy].astype(F32)
        b1[yy] = v.astype(BF16)
        if dy:
            cp = remote(b1.at[yy], s1.at[dy - 1], st2_s.at[1, dy - 1], st2_r.at[1, dy - 1], y_peer(dy))
            cp.start()
            st2.append(cp)
    for cp in st2:
        cp.wait_recv()
    v = b0[x].astype(F32)
    for i in range(3):
        v = v + s0[i].astype(F32)
    zs[0:8] = v.reshape(8, 16, 128).astype(BF16)
    v = b1[y].astype(F32)
    for i in range(3):
        v = v + s1[i].astype(F32)
    zs[8:16] = v.reshape(8, 16, 128).astype(BF16)
    zc = []
    for d in range(1, NZ):
        zz = lax.rem(z + d, NZ)
        cp = remote(zs.at[zz], zr.at[d - 1], z_s.at[d - 1], z_r.at[d - 1], z_peer(d))
        cp.start()
        zc.append(cp)

    for i in range(2):
        @pl.when(has[i])
        def _(i=i):
            back[1 - i].wait_recv()

        @pl.when(jnp.logical_not(has[i]))
        def _(i=i):
            pf[i] = jnp.zeros((ROWS, FEAT), BF16)

    def total(i, carry):
        rows = pl.ds(pl.multiple_of(i * STEP, STEP), STEP)
        own = pl.ds(pl.multiple_of(ROWS + i * STEP, STEP), STEP)
        v = pall[own].astype(F32) + pf[0, rows].astype(F32) + pf[1, rows].astype(F32)
        hgv[rows] = v.astype(BF16)
        return carry

    lax.fori_loop(0, ROWS // STEP, total, 0)
    ptot = hgv[...]
    for nb in range(4):
        cols = slice(nb * 256, (nb + 1) * 256)
        ov[:, cols] = dot_nt(ptot, wv[nb * 256 : (nb + 1) * 256]).astype(BF16)
    store = pltpu.make_async_copy(ov, hg_ref, store_sem.at[0])
    store.start()

    for cp in zc:
        cp.wait_recv()
    v = zs[z].astype(F32)
    for d in range(NZ - 1):
        v = v + zr[d].astype(F32)
    ag[k] = v * (1.0 / 1024.0)
    agc = []
    for d in range(1, NCLIP):
        cp = remote(ag.at[k], ag.at[k], ag_s.at[d - 1], ag_r.at[d - 1], clip_peer(d))
        cp.start()
        agc.append(cp)
    for cp in agc:
        cp.wait_recv()
    for i in range(NCLIP):
        wg_ref[:, i * 128 : (i + 1) * 128] = ag[i]

    for i in range(2):
        @pl.when(has[i])
        def _(i=i):
            for cp in halo[i]:
                cp.wait_send()
            back[i].wait_send()
    for cp in list(fwd.values()) + d2d + st1 + st1b + st2 + zc + agc:
        cp.wait_send()
    store.wait()


def local(student_hidden, teacher_tokens, proj_weight):
    dma = pltpu.SemaphoreType.DMA
    vm = pltpu.VMEM
    hidden_grad, weight_grad = pl.pallas_call(
        kernel,
        out_shape=(
            jax.ShapeDtypeStruct((ROWS, FEAT), BF16),
            jax.ShapeDtypeStruct((16, FEAT), F32),
        ),
        in_specs=[pl.BlockSpec(memory_space=pl.ANY)] * 3,
        out_specs=(pl.BlockSpec(memory_space=pl.ANY), pl.BlockSpec(memory_space=pltpu.VMEM)),
        scratch_shapes=[
            vm((FEAT, FEAT), BF16),
            vm((3, ROWS, FEAT), BF16),
            vm((3, ROWS, FEAT), BF16),
            vm((3, 2, ROWS, FEAT), BF16),
            vm((3, 2, ROWS, FEAT), BF16),
            vm((3, ROWS, FEAT), F32),
            vm((3, ROWS, 128), F32),
            vm((10, ROWS, ROWS), F32),
            vm((ROWS, 6 * ROWS), BF16),
            vm((2, ROWS, 2 * ROWS), BF16),
            vm((3, ROWS, FEAT), F32),
            vm((3 * ROWS, FEAT), BF16),
            vm((2, 512, 3 * ROWS), BF16),
            vm((4, 2, 512, 128), BF16),
            vm((4, 2, 512, 128), BF16),
            vm((4, 4, 128, 128), BF16),
            vm((4, 4, 128, 128), BF16),
            vm((3, 4, 128, 128), BF16),
            vm((3, 4, 128, 128), BF16),
            vm((4, 128, 128), BF16),
            vm((4, 128, 128), BF16),
            vm((3, 128, 128), BF16),
            vm((3, 128, 128), BF16),
            vm((NZ, 16, 128), BF16),
            vm((NZ - 1, 16, 128), BF16),
            vm((NCLIP, 16, 128), F32),
            vm((2, ROWS, FEAT), BF16),
            vm((ROWS, FEAT), BF16),
            vm((ROWS, FEAT), BF16),
            dma((3,)), dma((1,)),
            dma((2, 1 + HALF)), dma((2, 1 + HALF)),
            dma((2, 3)), dma((2, 3)),
            dma((2,)), dma((2,)),
            dma((4,)), dma((4,)),
            dma((3,)), dma((3,)),
            dma((3, 4)), dma((3, 4)),
            dma((2, 3)), dma((2, 3)),
            dma((NZ - 1,)), dma((NZ - 1,)),
            dma((NCLIP - 1,)), dma((NCLIP - 1,)),
        ],
        compiler_params=pltpu.CompilerParams(
            collective_id=0, has_side_effects=True, vmem_limit_bytes=56 * 2**20
        ),
    )(student_hidden[0], teacher_tokens[0], proj_weight)
    return hidden_grad[None], weight_grad


def solution(mesh):
    placed = (P("clip", "tok", None), P("clip", "tok", None), P())
    return jax.shard_map(
        local,
        mesh=mesh,
        in_specs=placed,
        out_specs=(P("clip", "tok", None), P("tok", None)),
        check_vma=False,
    )
```

```python
import jax
import jax.numpy as jnp
from jax import lax
from jax.experimental import pallas as pl
from jax.experimental.pallas import tpu as pltpu
from jax.sharding import PartitionSpec as P

EPSILON = 1e-06
MESH = pl.DeviceIdType.MESH
BF16 = jnp.bfloat16
F32 = jnp.float32
ROWS = 256
FEAT = 1024
NZ, NY, NX, NCLIP = 16, 4, 4, 8
CHAINS = 32
PARTS = 2
PART = ROWS // PARTS
FAR = ((0, 0), (0, 1), (2, 0), (2, 1))
STEP = 32


def dot_nn(a, b):
    return jnp.dot(a, b, preferred_element_type=F32)


def dot_nt(a, b):
    return lax.dot_general(a, b, (((1,), (1,)), ((), ())), preferred_element_type=F32)


def kernel(
    h_ref, t_ref, w_ref, hg_ref, wg_ref,
    wv, hr, tr, su, tu, proj, inv, ds, e_near, e_far, acc, pall, ht,
    early, ws, wr, a0, a1, r0, r1, b0, b1, s0, s1, zs, zr, ag, pf, hgv, ov,
    load_sem, store_sem, halo_s, halo_r, fwd_s, fwd_r, pf_s, pf_r,
    d2d_s, d2d_r, st1_s, st1_r, st1b_s, st1b_r, st2_s, st2_r, z_s, z_r, ag_s, ag_r,
):
    k = lax.axis_index("clip")
    b = lax.axis_index("tok")
    c = lax.rem(b, 2)
    q = b // 2
    z = lax.rem(q, NZ)
    xl = q // NZ
    y = k // 2
    xh = lax.rem(k, 2)
    x = xh * 2 + xl
    has = (q > 0, q < CHAINS - 1)
    turn = (q == NZ, q == NZ - 1)

    def at(yy, xx, zz, cc):
        return {"clip": yy * 2 + xx // 2, "tok": lax.rem(xx, 2) * 32 + zz * 2 + cc}

    sib = {"clip": k, "tok": b + 1 - 2 * c}
    side = ({"clip": k, "tok": b - 2}, {"clip": k, "tok": b + 2})

    def y_peer(d):
        return at(lax.rem(y + d, NY), x, z, c)

    def x_peer(d):
        return at(y, lax.rem(x + d, NX), z, c)

    def z_peer(d):
        return at(y, x, lax.rem(z + d, NZ), c)

    def clip_peer(d):
        return {"clip": lax.rem(k + d, NCLIP), "tok": b}

    def remote(src, dst, ssem, rsem, dev):
        return pltpu.make_async_remote_copy(
            src_ref=src, dst_ref=dst, send_sem=ssem, recv_sem=rsem, device_id=dev, device_id_type=MESH
        )

    loads = [
        pltpu.make_async_copy(h_ref, hr.at[1], load_sem.at[0]),
        pltpu.make_async_copy(t_ref, tr, load_sem.at[1]),
        pltpu.make_async_copy(w_ref, wv, load_sem.at[2]),
    ]
    for cp in loads:
        cp.start()
    barrier = pltpu.get_barrier_semaphore()

    def greet(dev):
        pl.semaphore_signal(barrier, inc=1, device_id=dev, device_id_type=MESH)

    greet(sib)
    for i in range(2):
        @pl.when(has[i])
        def _(i=i):
            greet(side[i])
    greet(x_peer(1))
    greet(x_peer(3))
    for d in range(1, NCLIP):
        greet(clip_peer(d))
    for d in range(1, NZ):
        greet(z_peer(d))
    ends = jnp.where(q > 0, 1, 0) + jnp.where(q < CHAINS - 1, 1, 0)

    def teacher_unit():
        def body(i, carry):
            rows = pl.ds(pl.multiple_of(i * STEP, STEP), STEP)
            v = tr[rows].astype(F32)
            r = lax.rsqrt(jnp.sum(v * v, axis=-1, keepdims=True) + EPSILON)
            tu[1, 0, rows] = (v * r).astype(BF16)
            return carry

        lax.fori_loop(0, ROWS // STEP, body, 0)

    def student_unit(slot, first, n):
        rows_all = slice(first, first + n)
        for nb in range(4):
            cols = slice(nb * 256, (nb + 1) * 256)
            proj[slot, rows_all, cols] = dot_nn(hr[slot, rows_all], wv[:, cols])

        def body(i, carry):
            rows = pl.ds(pl.multiple_of(first + i * STEP, STEP), STEP)
            v = proj[slot, rows]
            r = lax.rsqrt(jnp.sum(v * v, axis=-1, keepdims=True) + EPSILON)
            inv[slot, rows] = jnp.broadcast_to(r, (STEP, 128))
            su[slot, 0, rows] = (v * r).astype(BF16)
            return carry

        lax.fori_loop(0, n // STEP, body, 0)

    def transposed(slot):
        for j in range(4):
            cols = slice(j * 256, (j + 1) * 256)
            v = hr[slot, :, cols].astype(F32).T.reshape(8, 2, 16, ROWS)
            for cc in range(2):
                ht[cc, j * 128 : (j + 1) * 128, slot * 256 : (slot + 1) * 256] = (
                    v[:, cc].reshape(128, ROWS).astype(BF16)
                )

    loads[0].wait()
    pl.semaphore_wait(barrier, 3 + (NCLIP - 1) + (NZ - 1) + ends)

    def part(n):
        return pl.ds(n * PART, PART)

    def halo_copies(i):
        slot = 2 - 2 * i
        copies = []
        for n in range(PARTS):
            copies.append(
                remote(hr.at[1, part(n)], hr.at[slot, part(n)], halo_s.at[i, n], halo_r.at[i, n], side[i])
            )
        for n in range(PARTS):
            m = PARTS + n
            copies.append(
                remote(tu.at[1, 0, part(n)], tu.at[slot, 0, part(n)], halo_s.at[i, m], halo_r.at[i, m], side[i])
            )
        return copies

    halo = [halo_copies(0), halo_copies(1)]

    def halo_send(n):
        for i in range(2):
            @pl.when(has[i])
            def _(i=i):
                halo[i][n].start()

    def halo_arrival(slot, n):
        i = slot // 2

        @pl.when(has[i])
        def _():
            halo[1 - i][n].wait_recv()

        @pl.when(jnp.logical_not(has[i]))
        def _():
            if n < PARTS:
                hr[slot, n * PART : (n + 1) * PART] = jnp.zeros((PART, FEAT), BF16)
            else:
                tu[slot, 0, (n - PARTS) * PART : (n - PARTS + 1) * PART] = jnp.zeros((PART, FEAT), BF16)

    for n in range(PARTS):
        halo_send(n)
    loads[1].wait()
    teacher_unit()
    for n in range(PARTS):
        halo_send(PARTS + n)
    loads[2].wait()
    student_unit(1, 0, ROWS)

    fwd = []

    def forward(src, dst, n):
        cp = remote(src, dst, fwd_s.at[n], fwd_r.at[n], sib)
        cp.start()
        fwd.append(cp)
        return cp

    own_fwd = [
        forward(tu.at[1, 0], tu.at[1, 1], 0),
        forward(su.at[1, 0], su.at[1, 1], 1),
    ]
    transposed(1)
    for cp in own_fwd:
        cp.wait_recv()

    acc[...] = jnp.zeros_like(acc)

    def weigh(slot, student, teacher):
        w = (256.0 * (student - teacher)).astype(BF16)
        p = w.astype(F32) * student
        s = p[:, :128]
        if p.shape[1] == 256:
            s = s + p[:, 128:]
        acc[slot] = acc[slot] + s
        return w

    for who in range(2):
        e_near[:, who * 256 : (who + 1) * 256] = weigh(
            1, dot_nt(su[1, 0], su[1, who]), dot_nt(tu[1, 0], tu[1, who])
        )

    s_fwd = []
    for n in range(PARTS):
        for slot in (0, 2):
            halo_arrival(slot, n)
            student_unit(slot, n * PART, PART)
            if n == PARTS - 1:
                s_fwd.append(forward(su.at[slot, 0], su.at[slot, 1], 2 + slot // 2))
    for slot in (0, 2):
        transposed(slot)
    for cp in s_fwd:
        cp.wait_recv()
    for j, (slot, who) in enumerate(FAR):
        ds[j] = dot_nt(su[1, 0], su[slot, who])
    for f in range(2):
        ds[4 + f] = dot_nt(su[2 * f, 0], su[2 - 2 * f, 0])
    xs = 2 - 2 * c
    xo = 2 * c
    ds[6] = dot_nt(su[xs, 0], su[xo, 1])

    def near_part(j, n):
        slot, who = FAR[j]
        lo = 512 + n * 4 * PART + j * PART
        e_near[:, lo : lo + PART] = weigh(
            1, ds[j, :, n * PART : (n + 1) * PART], dot_nt(tu[1, 0], tu[slot, who, n * PART : (n + 1) * PART])
        )

    def near_rows(n, cols):
        return jnp.concatenate([su[slot, who, n * PART : (n + 1) * PART, cols] for slot, who in FAR], axis=0)

    t_fwd = []
    for n in range(PARTS):
        for slot in (0, 2):
            halo_arrival(slot, PARTS + n)
            t_fwd.append(
                forward(tu.at[slot, 0, part(n)], tu.at[slot, 1, part(n)], 4 + n * 2 + slot // 2)
            )
        for j in (0, 2):
            near_part(j, n)
        if n == PARTS - 1:
            for f in range(2):
                e_far[f] = weigh(2 * f, ds[4 + f], dot_nt(tu[2 * f, 0], tu[2 - 2 * f, 0]))
        for cp in t_fwd[2 * n : 2 * n + 2]:
            cp.wait_recv()
        for j in (1, 3):
            near_part(j, n)
        if n == 0:
            for nb in range(4):
                cols = slice(nb * 256, (nb + 1) * 256)
                early[nb] = dot_nn(e_near[:, 0:512], su[1, :, :, cols].reshape(512, 256)) + dot_nn(
                    e_near[:, 512:1024], near_rows(0, cols)
                )
    e_far[2] = weigh(xs, ds[6], dot_nt(tu[xs, 0], tu[xo, 1]))

    def finish_along(i, carry):
        for slot in range(3):
            rows = pl.ds(pl.multiple_of(i * 64, 64), 64)
            along = jnp.sum(acc[slot, rows], axis=-1, keepdims=True)
            acc[slot, rows] = along * inv[slot, rows]
        return carry

    lax.fori_loop(0, ROWS // 64, finish_along, 0)

    back = [[None] * 4 for _ in range(2)]
    d2d, st1, st1b = [], [], []

    sent_first = (0, 1, 2)

    def send_turn(ds_):
        for i in range(2):
            @pl.when(turn[i])
            def _(i=i):
                for d in ds_:
                    back[i][d].start()

    def gradient(d):
        yy = lax.rem(y + 1 + d, NY)
        cols = pl.ds(pl.multiple_of(yy * 256, 256), 256)
        grads = {
            1: early[yy] + dot_nn(e_near[:, 1024:1536], near_rows(1, cols)),
            0: dot_nn(e_far[0], su[2, 0, :, cols]),
            2: dot_nn(e_far[1], su[0, 0, :, cols]),
        }
        cross = dot_nn(e_far[2], su[xo, 1, :, cols])
        first = jnp.where(c == 1, 1.0, 0.0)
        grads[0] = grads[0] + first * cross
        grads[2] = grads[2] + (1.0 - first) * cross
        for slot in (0, 2, 1):
            for i in range(2):
                at_cols = pl.ds(pl.multiple_of(yy * 256 + i * 128, 128), 128)
                v = grads[slot][:, i * 128 : (i + 1) * 128]
                v = (v - proj[slot, :, at_cols] * acc[slot]) * inv[slot]
                pall[yy, slot * ROWS : (slot + 1) * ROWS, i * 128 : (i + 1) * 128] = v.astype(BF16)
        for i in range(2):
            back[i][d] = remote(
                pall.at[yy, pl.ds(2 * i * ROWS, ROWS)], pf.at[1 - i, yy], pf_s.at[i, d], pf_r.at[i, d], side[i]
            )
            if d in sent_first:
                go = has[i]
            else:
                go = jnp.logical_and(has[i], jnp.logical_not(turn[i]))

            @pl.when(go)
            def _(i=i):
                back[i][d].start()

    def weight_sibling(d):
        yy = lax.rem(y + 1 + d, NY)
        part_sib = dot_nn(ht[1 - c], pall[yy])
        for i in range(2):
            ws[d, i] = part_sib[:, i * 128 : (i + 1) * 128].astype(BF16)
        cp = remote(ws.at[d], wr.at[d], d2d_s.at[d], d2d_r.at[d], sib)
        cp.start()
        d2d.append(cp)

    def reduce_first(d):
        dy = (1 + d) % 4
        yy = lax.rem(y + dy, NY)
        part_own = dot_nn(ht[c], pall[yy])
        d2d[d].wait_recv()
        for i in range(2):
            v = (part_own[:, i * 128 : (i + 1) * 128] + wr[d, i].astype(F32)).astype(BF16)
            for j in range(2):
                a0[yy, i * 2 + j] = v[j * 256 : j * 256 + 128]
                a1[i * 2 + j, yy] = v[j * 256 + 128 : j * 256 + 256]
        if dy:
            cp = remote(a0.at[yy], r0.at[dy - 1], st1_s.at[dy - 1], st1_r.at[dy - 1], y_peer(dy))
            cp.start()
            st1.append(cp)
        for dx in range(1, NX):
            xx = lax.rem(x + dx, NX)
            cp = remote(
                a1.at[xx, yy], r1.at[dx - 1, yy], st1b_s.at[dx - 1, dy], st1b_r.at[dx - 1, dy], x_peer(dx)
            )
            cp.start()
            st1b.append(cp)

    gradient(0)
    weight_sibling(0)
    for d in range(2):
        gradient(d + 1)
        reduce_first(d)
        weight_sibling(d + 1)
    gradient(3)
    weight_sibling(3)
    reduce_first(2)
    reduce_first(3)

    st2 = []
    for cp in st1:
        cp.wait_recv()
    for dx in (1, 2, 3, 0):
        xx = lax.rem(x + dx, NX)
        v = a0[y, xx].astype(F32)
        for i in range(3):
            v = v + r0[i, xx].astype(F32)
        b0[xx] = v.astype(BF16)
        if dx:
            cp = remote(b0.at[xx], s0.at[dx - 1], st2_s.at[0, dx - 1], st2_r.at[0, dx - 1], x_peer(dx))
            cp.start()
            st2.append(cp)
    for cp in st1b:
        cp.wait_recv()
    send_turn(())
    for dy in (1, 2, 3, 0):
        yy = lax.rem(y + dy, NY)
        v = a1[x, yy].astype(F32)
        for i in range(3):
            v = v + r1[i, yy].astype(F32)
        b1[yy] = v.astype(BF16)
        if dy:
            cp = remote(b1.at[yy], s1.at[dy - 1], st2_s.at[1, dy - 1], st2_r.at[1, dy - 1], y_peer(dy))
            cp.start()
            st2.append(cp)
    def over_z(half, own, got, copies):
        for cp in copies:
            cp.wait_recv()
        v = own.astype(F32)
        for i in range(3):
            v = v + got[i].astype(F32)
        zs[half * 8 : half * 8 + 8] = v.reshape(8, 16, 128).astype(BF16)
        for zz in range(half * 8, half * 8 + 8):
            cp = remote(zs.at[zz], zr.at[z], z_s.at[zz], z_r.at[z], at(y, x, zz, c))
            zc.append(cp)

            @pl.when(z != zz)
            def _(cp=cp):
                cp.start()

    zc = []
    over_z(0, b0[x], s0, st2[:3])
    over_z(1, b1[y], s1, st2[3:])
    send_turn((3,))
    zr[z] = zs[z]

    def hidden_gradient():
        for i in range(2):
            @pl.when(has[i])
            def _(i=i):
                for d in range(4):
                    back[1 - i][d].wait_recv()

            @pl.when(jnp.logical_not(has[i]))
            def _(i=i):
                pf[i] = jnp.zeros((4, ROWS, 256), BF16)

        for nb in range(4):
            v = pall[nb, ROWS : 2 * ROWS].astype(F32) + pf[0, nb].astype(F32) + pf[1, nb].astype(F32)
            hgv[:, nb * 256 : (nb + 1) * 256] = v.astype(BF16)
        for nb in range(4):
            cols = slice(nb * 256, (nb + 1) * 256)
            ov[:, cols] = dot_nt(hgv[...], wv[nb * 256 : (nb + 1) * 256]).astype(BF16)

    def weight_gather():
        for zz in range(NZ):
            @pl.when(z != zz)
            def _(zz=zz):
                remote(zs.at[zz], zr.at[zz], z_s.at[zz], z_r.at[zz], at(y, x, zz, c)).wait_recv()

        v = zr[0].astype(F32)
        for zz in range(1, NZ):
            v = v + zr[zz].astype(F32)
        ag[k] = v * (1.0 / 1024.0)
        copies = []
        for d in range(1, NCLIP):
            cp = remote(ag.at[k], ag.at[k], ag_s.at[d - 1], ag_r.at[d - 1], clip_peer(d))
            cp.start()
            copies.append(cp)
        return copies

    agc = weight_gather()
    hidden_gradient()
    store = pltpu.make_async_copy(ov, hg_ref, store_sem.at[0])
    store.start()
    for cp in agc:
        cp.wait_recv()
    for i in range(NCLIP):
        wg_ref[:, i * 128 : (i + 1) * 128] = ag[i]

    for i in range(2):
        @pl.when(has[i])
        def _(i=i):
            for cp in halo[i] + back[i]:
                cp.wait_send()
    for zz in range(NZ):
        @pl.when(z != zz)
        def _(zz=zz):
            zc[zz].wait_send()

    for cp in fwd + d2d + st1 + st1b + st2 + agc:
        cp.wait_send()
    store.wait()


def handed_on(hg_in, wg_in, hg_out, wg_out):
    hg_out[...] = hg_in[...]
    wg_out[...] = wg_in[...]


def local(student_hidden, teacher_tokens, proj_weight):
    dma = pltpu.SemaphoreType.DMA
    vm = pltpu.VMEM
    anywhere = pl.BlockSpec(memory_space=pl.ANY)
    results = (
        jax.ShapeDtypeStruct((ROWS, FEAT), BF16),
        jax.ShapeDtypeStruct((16, FEAT), F32),
    )
    made = pl.pallas_call(
        kernel,
        out_shape=results,
        in_specs=[anywhere] * 3,
        out_specs=(anywhere, pl.BlockSpec(memory_space=pltpu.VMEM)),
        scratch_shapes=[
            vm((FEAT, FEAT), BF16),
            vm((3, ROWS, FEAT), BF16),
            vm((ROWS, FEAT), BF16),
            vm((3, 2, ROWS, FEAT), BF16),
            vm((3, 2, ROWS, FEAT), BF16),
            vm((3, ROWS, FEAT), F32),
            vm((3, ROWS, 128), F32),
            vm((7, ROWS, ROWS), F32),
            vm((ROWS, 6 * ROWS), BF16),
            vm((3, ROWS, ROWS), BF16),
            vm((3, ROWS, 128), F32),
            vm((4, 3 * ROWS, 256), BF16),
            vm((2, 512, 3 * ROWS), BF16),
            vm((4, ROWS, 256), F32),
            vm((4, 2, 512, 128), BF16),
            vm((4, 2, 512, 128), BF16),
            vm((4, 4, 128, 128), BF16),
            vm((4, 4, 128, 128), BF16),
            vm((3, 4, 128, 128), BF16),
            vm((3, 4, 128, 128), BF16),
            vm((4, 128, 128), BF16),
            vm((4, 128, 128), BF16),
            vm((3, 128, 128), BF16),
            vm((3, 128, 128), BF16),
            vm((NZ, 16, 128), BF16),
            vm((NZ, 16, 128), BF16),
            vm((NCLIP, 16, 128), F32),
            vm((2, 4, ROWS, 256), BF16),
            vm((ROWS, FEAT), BF16),
            vm((ROWS, FEAT), BF16),
            dma((3,)), dma((1,)),
            dma((2, 2 * PARTS)), dma((2, 2 * PARTS)),
            dma((4 + 2 * PARTS,)), dma((4 + 2 * PARTS,)),
            dma((2, 4)), dma((2, 4)),
            dma((4,)), dma((4,)),
            dma((3,)), dma((3,)),
            dma((3, 4)), dma((3, 4)),
            dma((2, 3)), dma((2, 3)),
            dma((NZ,)), dma((NZ,)),
            dma((NCLIP - 1,)), dma((NCLIP - 1,)),
        ],
        compiler_params=pltpu.CompilerParams(
            collective_id=0, has_side_effects=True, vmem_limit_bytes=56 * 2**20
        ),
    )(student_hidden[0], teacher_tokens[0], proj_weight)
    hidden_grad, weight_grad = pl.pallas_call(
        handed_on,
        out_shape=results,
        in_specs=[pl.BlockSpec(memory_space=pltpu.VMEM)] * 2,
        out_specs=(pl.BlockSpec(memory_space=pltpu.VMEM),) * 2,
    )(*made)
    return hidden_grad[None], weight_grad


def solution(mesh):
    placed = (P("clip", "tok", None), P("clip", "tok", None), P())
    return jax.shard_map(
        local,
        mesh=mesh,
        in_specs=placed,
        out_specs=(P("clip", "tok", None), P("tok", None)),
        check_vma=False,
    )
```

```python
import jax
import jax.numpy as jnp
from jax import lax
from jax.experimental import pallas as pl
from jax.experimental.pallas import tpu as pltpu
from jax.sharding import PartitionSpec as P

EPSILON = 1e-06
MESH = pl.DeviceIdType.MESH
BF16 = jnp.bfloat16
F32 = jnp.float32
ROWS = 256
FEAT = 1024
NZ, NY, NX, NCLIP = 16, 4, 4, 8
CHAINS = 32
PARTS = 2
PART = ROWS // PARTS
WORDS = 7
FAR = ((0, 0), (0, 1), (2, 0), (2, 1))
STEP = 32


def dot_nn(a, b):
    return jnp.dot(a, b, preferred_element_type=F32)


def dot_nt(a, b):
    return lax.dot_general(a, b, (((1,), (1,)), ((), ())), preferred_element_type=F32)


def kernel(
    h_ref, t_ref, w_ref, hg_ref, wg_ref,
    wv, hr, tr, su, tu, proj, inv, ds, e_near, e_far, acc, pall, ht,
    early, ws, wr, a0, a1, r0, r1, b0, b1, s0, s1, zs, zr, ag, pf, hgv, ov,
    load_sem, store_sem, halo_s, halo_r, fwd_s, fwd_r, pf_s, pf_r,
    d2d_s, d2d_r, st1_s, st1_r, st1b_s, st1b_r, st2_s, st2_r, z_s, z_r, ag_s, ag_r, word,
):
    k = lax.axis_index("clip")
    b = lax.axis_index("tok")
    c = lax.rem(b, 2)
    q = b // 2
    z = lax.rem(q, NZ)
    xl = q // NZ
    y = k // 2
    xh = lax.rem(k, 2)
    x = xh * 2 + xl
    has = (q > 0, q < CHAINS - 1)
    turn = (q == NZ, q == NZ - 1)
    corner = (2 * CHAINS - 2 + c, c)

    def at(yy, xx, zz, cc):
        return {"clip": yy * 2 + xx // 2, "tok": lax.rem(xx, 2) * 32 + zz * 2 + cc}

    sib = {"clip": k, "tok": b + 1 - 2 * c}
    side = ({"clip": k, "tok": b - 2}, {"clip": k, "tok": b + 2})

    def y_peer(d):
        return at(lax.rem(y + d, NY), x, z, c)

    def x_peer(d):
        return at(y, lax.rem(x + d, NX), z, c)

    def z_peer(d):
        return at(y, x, lax.rem(z + d, NZ), c)

    def remote(src, dst, ssem, rsem, dev):
        return pltpu.make_async_remote_copy(
            src_ref=src, dst_ref=dst, send_sem=ssem, recv_sem=rsem, device_id=dev, device_id_type=MESH
        )

    loads = [
        pltpu.make_async_copy(h_ref, hr.at[1], load_sem.at[0]),
        pltpu.make_async_copy(t_ref, tr, load_sem.at[1]),
        pltpu.make_async_copy(w_ref, wv, load_sem.at[2]),
    ]
    for cp in loads:
        cp.start()
    barrier = pltpu.get_barrier_semaphore()

    def greet(dev):
        pl.semaphore_signal(barrier, inc=1, device_id=dev, device_id_type=MESH)

    near_peers = (
        at(y, x, lax.rem(z + 1, NZ), c), at(y, x, lax.rem(z + NZ - 1, NZ), c),
        y_peer(1), y_peer(NY - 1), x_peer(1), x_peer(NX - 1),
    )
    for i in range(2):
        @pl.when(has[i])
        def _(i=i):
            greet(side[i])
    greet(sib)
    for dev in near_peers:
        greet(dev)
    ends = jnp.where(q > 0, 1, 0) + jnp.where(q < CHAINS - 1, 1, 0)

    def heard(n):
        for i in range(len(near_peers)):
            pl.semaphore_wait(word.at[n, i], 1)

    def pass_on(n):
        if n:
            heard(n - 1)
        for i, dev in enumerate(near_peers):
            pl.semaphore_signal(word.at[n, i], inc=1, device_id=dev, device_id_type=MESH)

    def teacher_unit():
        def body(i, carry):
            rows = pl.ds(pl.multiple_of(i * STEP, STEP), STEP)
            v = tr[rows].astype(F32)
            r = lax.rsqrt(jnp.sum(v * v, axis=-1, keepdims=True) + EPSILON)
            tu[1, 0, rows] = (v * r).astype(BF16)
            return carry

        lax.fori_loop(0, ROWS // STEP, body, 0)

    def student_unit(slot, first, n):
        rows_all = slice(first, first + n)

        def block(nb, carry):
            cols = pl.ds(pl.multiple_of(nb * 256, 256), 256)
            proj[slot, rows_all, cols] = dot_nn(hr[slot, rows_all], wv[:, cols])
            return carry

        lax.fori_loop(0, 4, block, 0)

        def body(i, carry):
            rows = pl.ds(pl.multiple_of(first + i * STEP, STEP), STEP)
            v = proj[slot, rows]
            r = lax.rsqrt(jnp.sum(v * v, axis=-1, keepdims=True) + EPSILON)
            inv[slot, rows] = jnp.broadcast_to(r, (STEP, 128))
            su[slot, 0, rows] = (v * r).astype(BF16)
            return carry

        lax.fori_loop(0, n // STEP, body, 0)

    def transposed(slot):
        for j in range(4):
            cols = slice(j * 256, (j + 1) * 256)
            v = hr[slot, :, cols].astype(F32).T.reshape(8, 2, 16, ROWS)
            for cc in range(2):
                ht[cc, j * 128 : (j + 1) * 128, slot * 256 : (slot + 1) * 256] = (
                    v[:, cc].reshape(128, ROWS).astype(BF16)
                )

    loads[0].wait()
    pl.semaphore_wait(barrier, 1 + len(near_peers) + ends)

    def part(n):
        return pl.ds(n * PART, PART)

    def halo_copy(i, n):
        slot = 2 - 2 * i
        sems = (halo_s.at[i, n], halo_r.at[i, n], side[i])
        if isinstance(n, int) and n < PARTS:
            return remote(hr.at[1, part(n)], hr.at[slot, part(n)], *sems)
        rows = pl.ds(pl.multiple_of((n - PARTS) * PART, PART), PART)
        return remote(tu.at[1, 0, rows], tu.at[slot, 0, rows], *sems)

    halo = [[halo_copy(i, n) for n in range(2 * PARTS)] for i in range(2)]

    def halo_send(n):
        for i in range(2):
            @pl.when(has[i])
            def _(i=i):
                halo[i][n].start()

    def halo_arrival(slot, n):
        i = slot // 2

        @pl.when(has[i])
        def _():
            halo[1 - i][n].wait_recv()

        @pl.when(jnp.logical_not(has[i]))
        def _():
            hr[slot, n * PART : (n + 1) * PART] = jnp.zeros((PART, FEAT), BF16)

    for n in range(PARTS):
        halo_send(n)
    pass_on(0)
    loads[1].wait()
    teacher_unit()
    for n in range(PARTS):
        halo_send(PARTS + n)
    loads[2].wait()
    student_unit(1, 0, ROWS)
    pass_on(1)

    fwd = []

    def forward(src, dst, n):
        cp = remote(src, dst, fwd_s.at[n], fwd_r.at[n], sib)
        cp.start()
        fwd.append(cp)
        return cp

    own_fwd = [
        forward(tu.at[1, 0], tu.at[1, 1], 0),
        forward(su.at[1, 0], su.at[1, 1], 1),
    ]
    transposed(1)
    for cp in own_fwd:
        cp.wait_recv()

    acc[...] = jnp.zeros_like(acc)

    def weigh(slot, student, teacher):
        w = (256.0 * (student - teacher)).astype(BF16)
        p = w.astype(F32) * student
        s = p[:, :128]
        if p.shape[1] == 256:
            s = s + p[:, 128:]
        acc[slot] = acc[slot] + s
        return w

    for who in range(2):
        e_near[:, who * 256 : (who + 1) * 256] = weigh(
            1, dot_nt(su[1, 0], su[1, who]), dot_nt(tu[1, 0], tu[1, who])
        )

    pass_on(2)

    s_fwd = []
    for n in range(PARTS):
        for slot in (0, 2):
            halo_arrival(slot, n)
            student_unit(slot, n * PART, PART)
            if n == PARTS - 1:
                s_fwd.append(forward(su.at[slot, 0], su.at[slot, 1], 2 + slot // 2))
            pass_on(3 + n * 2 + slot // 2)
    for slot in (0, 2):
        transposed(slot)
    for cp in s_fwd:
        cp.wait_recv()
    xs = 2 - 2 * c
    xo = 2 * c

    def far_pair(f):
        rows = jnp.where(f == 2, xs, 2 * f)
        return rows, 2 - rows, jnp.where(f == 2, 1, 0)

    def near_student(j, carry):
        ds[j] = dot_nt(su[1, 0], su[(j // 2) * 2, lax.rem(j, 2)])
        return carry

    lax.fori_loop(0, 4, near_student, 0)

    def far_student(f, carry):
        rows, slot, who = far_pair(f)
        ds[4 + f] = dot_nt(su[rows, 0], su[slot, who])
        return carry

    lax.fori_loop(0, 3, far_student, 0)

    def near_part(j, n):
        at_rows = pl.ds(pl.multiple_of(n * PART, PART), PART)
        e_near[:, pl.ds(pl.multiple_of(512 + n * 4 * PART + j * PART, PART), PART)] = weigh(
            1, ds[j, :, at_rows], dot_nt(tu[1, 0], tu[(j // 2) * 2, lax.rem(j, 2), at_rows])
        )

    def near_rows(n, cols):
        return jnp.concatenate([su[slot, who, n * PART : (n + 1) * PART, cols] for slot, who in FAR], axis=0)

    def teacher_part(n, carry):
        def arrived(slot):
            i = slot // 2
            rows = pl.ds(pl.multiple_of(n * PART, PART), PART)

            @pl.when(has[i])
            def _():
                halo_copy(1 - i, PARTS + n).wait_recv()

            @pl.when(jnp.logical_not(has[i]))
            def _():
                tu[slot, 0, rows] = jnp.zeros((PART, FEAT), BF16)

            cp = teacher_forward(slot, n)
            cp.start()
            return cp

        copies = [arrived(0), arrived(2)]

        def direct(j, cc):
            near_part(2 * j, n)
            return cc

        def handed(j, cc):
            near_part(2 * j + 1, n)
            return cc

        lax.fori_loop(0, 2, direct, 0)

        @pl.when(n == PARTS - 1)
        def _():
            lax.fori_loop(0, 2, far_weight, 0)

        for cp in copies:
            cp.wait_recv()
        lax.fori_loop(0, 2, handed, 0)

        @pl.when(n == 0)
        def _():
            def block(nb, cc):
                cols = pl.ds(pl.multiple_of(nb * 256, 256), 256)
                early[nb] = dot_nn(e_near[:, 0:512], su[1, :, :, cols].reshape(512, 256)) + dot_nn(
                    e_near[:, 512:1024], near_rows(0, cols)
                )
                return cc

            lax.fori_loop(0, 4, block, 0)

        return carry

    def teacher_forward(slot, n):
        rows = pl.ds(pl.multiple_of(n * PART, PART), PART)
        m = 4 + n * 2 + slot // 2
        return remote(tu.at[slot, 0, rows], tu.at[slot, 1, rows], fwd_s.at[m], fwd_r.at[m], sib)

    def far_weight(f, carry):
        rows, slot, who = far_pair(f)
        e_far[f] = weigh(rows, ds[4 + f], dot_nt(tu[rows, 0], tu[slot, who]))
        return carry

    lax.fori_loop(0, PARTS, teacher_part, 0)
    far_weight(2, 0)
    for n in range(PARTS):
        for slot in (0, 2):
            fwd.append(teacher_forward(slot, n))

    def finish_along(i, carry):
        for slot in range(3):
            rows = pl.ds(pl.multiple_of(i * 64, 64), 64)
            along = jnp.sum(acc[slot, rows], axis=-1, keepdims=True)
            acc[slot, rows] = along * inv[slot, rows]
        return carry

    lax.fori_loop(0, ROWS // 64, finish_along, 0)

    heard(WORDS - 1)

    def offset(d):
        return jnp.where(d == 0, 2, jnp.where(d == 1, 1, jnp.where(d == 2, 3, 0)))

    def chunk(d):
        return lax.rem(y + offset(d), NY)

    def back_copy(i, d):
        yy = chunk(d)
        dev = {"clip": k, "tok": jnp.where(jnp.logical_and(turn[i], lax.rem(d, 2) == 1), corner[i], b + 4 * i - 2)}
        return remote(
            pall.at[yy, pl.ds(2 * i * ROWS, ROWS)], pf.at[1 - i, yy], pf_s.at[i, d], pf_r.at[i, d], dev
        )

    def relay_copy(i, d):
        yy = chunk(d)
        dev = {"clip": k, "tok": jnp.where(xl == 0, b + 32, b - 32)}
        return remote(pf.at[i, yy], pf.at[i, yy], pf_s.at[i, d], pf_r.at[1 - i, d], dev)

    def relay(d):
        for i in range(2):
            @pl.when(jnp.logical_not(has[i]))
            def _(i=i):
                relay_copy(i, d).wait_recv()
                relay_copy(i, d).start()

    def d2d_copy(d):
        return remote(ws.at[d], wr.at[d], d2d_s.at[d], d2d_r.at[d], sib)

    def first_y(d):
        return remote(a0.at[chunk(d)], r0.at[d], st1_s.at[d], st1_r.at[d], y_peer(offset(d)))

    def first_x(dx, d):
        yy = chunk(d)
        return remote(
            a1.at[lax.rem(x + dx, NX), yy], r1.at[dx - 1, yy], st1b_s.at[dx - 1, d], st1b_r.at[dx - 1, d], x_peer(dx)
        )

    def gradient(d):
        yy = chunk(d)
        cols = pl.ds(pl.multiple_of(yy * 256, 256), 256)
        grads = {
            1: early[yy] + dot_nn(e_near[:, 1024:1536], near_rows(1, cols)),
            0: dot_nn(e_far[0], su[2, 0, :, cols]),
            2: dot_nn(e_far[1], su[0, 0, :, cols]),
        }
        cross = dot_nn(e_far[2], su[xo, 1, :, cols])
        first = jnp.where(c == 1, 1.0, 0.0)
        grads[0] = grads[0] + first * cross
        grads[2] = grads[2] + (1.0 - first) * cross
        for slot in (0, 2, 1):
            for i in range(2):
                at_cols = pl.ds(pl.multiple_of(yy * 256 + i * 128, 128), 128)
                v = grads[slot][:, i * 128 : (i + 1) * 128]
                v = (v - proj[slot, :, at_cols] * acc[slot]) * inv[slot]
                pall[yy, slot * ROWS : (slot + 1) * ROWS, i * 128 : (i + 1) * 128] = v.astype(BF16)
        for i in range(2):
            @pl.when(has[i])
            def _(i=i):
                back_copy(i, d).start()

    def weight_sibling(d):
        part_sib = dot_nn(ht[1 - c], pall[chunk(d)])
        for i in range(2):
            ws[d, i] = part_sib[:, i * 128 : (i + 1) * 128].astype(BF16)
        d2d_copy(d).start()

    def reduce_first(d):
        yy = chunk(d)
        part_own = dot_nn(ht[c], pall[yy])
        d2d_copy(d).wait_recv()
        for i in range(2):
            v = (part_own[:, i * 128 : (i + 1) * 128] + wr[d, i].astype(F32)).astype(BF16)
            for j in range(2):
                a0[yy, i * 2 + j] = v[j * 256 : j * 256 + 128]
                a1[i * 2 + j, yy] = v[j * 256 + 128 : j * 256 + 256]

        @pl.when(d < 3)
        def _():
            first_y(d).start()

        for dx in (2, 1, 3):
            first_x(dx, d).start()

    def step(s, carry):
        @pl.when(s < 4)
        def _():
            gradient(s)
            weight_sibling(s)

        @pl.when(s > 0)
        def _():
            reduce_first(s - 1)

        return carry

    lax.fori_loop(0, 5, step, 0)
    back = [[back_copy(i, d) for d in range(4)] for i in range(2)]
    d2d = [d2d_copy(d) for d in range(4)]
    st1 = [first_y(d) for d in range(3)]
    st1b = [first_x(dx, d) for dx in (1, 2, 3) for d in range(4)]

    relay(1)
    st2 = []
    for cp in st1:
        cp.wait_recv()
    for dx in (2, 1, 3, 0):
        xx = lax.rem(x + dx, NX)
        v = a0[y, xx].astype(F32)
        for i in range(3):
            v = v + r0[i, xx].astype(F32)
        b0[xx] = v.astype(BF16)
        if dx:
            cp = remote(b0.at[xx], s0.at[dx - 1], st2_s.at[0, dx - 1], st2_r.at[0, dx - 1], x_peer(dx))
            cp.start()
            st2.append(cp)
    for cp in st1b:
        cp.wait_recv()
    relay(3)
    for dy in (2, 1, 3, 0):
        yy = lax.rem(y + dy, NY)
        v = a1[x, yy].astype(F32)
        for i in range(3):
            v = v + r1[i, yy].astype(F32)
        b1[yy] = v.astype(BF16)
        if dy:
            cp = remote(b1.at[yy], s1.at[dy - 1], st2_s.at[1, dy - 1], st2_r.at[1, dy - 1], y_peer(dy))
            cp.start()
            st2.append(cp)
    for cp in st2:
        cp.wait_recv()
    for half, own, got in ((0, b0[x], s0), (1, b1[y], s1)):
        v = own.astype(F32)
        for i in range(3):
            v = v + got[i].astype(F32)
        zs[half * 8 : half * 8 + 8] = v.reshape(8, 16, 128).astype(BF16)
    zc = []
    for d in (8, 7, 9, 6, 10, 5, 11, 4, 12, 3, 13, 2, 14, 1, 15):
        cp = remote(zs.at[lax.rem(z + d, NZ)], zr.at[d - 1], z_s.at[d - 1], z_r.at[d - 1], z_peer(d))
        cp.start()
        zc.append(cp)

    def hidden_gradient():
        for i in range(2):
            @pl.when(has[i])
            def _(i=i):
                for d in range(4):
                    back[1 - i][d].wait_recv()

            @pl.when(jnp.logical_not(has[i]))
            def _(i=i):
                for d in (1, 3):
                    relay_copy(i, d).wait_send()
                pf[i] = jnp.zeros((4, ROWS, 256), BF16)

        for nb in range(4):
            v = pall[nb, ROWS : 2 * ROWS].astype(F32) + pf[0, nb].astype(F32) + pf[1, nb].astype(F32)
            hgv[:, nb * 256 : (nb + 1) * 256] = v.astype(BF16)

        def block(nb, carry):
            at_block = pl.ds(pl.multiple_of(nb * 256, 256), 256)
            ov[:, at_block] = dot_nt(hgv[...], wv[at_block]).astype(BF16)
            return carry

        lax.fori_loop(0, 4, block, 0)

    def weight_gather():
        v = zs[z].astype(F32)
        for cp in zc:
            cp.wait_recv()
        for d in range(NZ - 1):
            v = v + zr[d].astype(F32)
        ag[k] = v * (1.0 / 1024.0)
        copies = []
        for n, (dy, dh) in enumerate(((2, 1), (1, 1), (3, 1), (2, 0), (0, 1), (1, 0), (3, 0))):
            dev = {"clip": lax.rem(y + dy, NY) * 2 + (1 - xh if dh else xh), "tok": b}
            cp = remote(ag.at[k], ag.at[k], ag_s.at[n], ag_r.at[n], dev)
            cp.start()
            copies.append(cp)
        return copies

    agc = weight_gather()
    hidden_gradient()
    store = pltpu.make_async_copy(ov, hg_ref, store_sem.at[0])
    store.start()
    for cp in agc:
        cp.wait_recv()
    for i in range(NCLIP):
        wg_ref[:, i * 128 : (i + 1) * 128] = ag[i]

    for i in range(2):
        @pl.when(has[i])
        def _(i=i):
            for cp in halo[i] + back[i]:
                cp.wait_send()
    for cp in fwd + d2d + st1 + st1b + st2 + zc + agc:
        cp.wait_send()
    store.wait()


def handed_on(hg_in, wg_in, hg_out, wg_out):
    hg_out[...] = hg_in[...]
    wg_out[...] = wg_in[...]


def local(student_hidden, teacher_tokens, proj_weight):
    dma = pltpu.SemaphoreType.DMA
    vm = pltpu.VMEM
    anywhere = pl.BlockSpec(memory_space=pl.ANY)
    results = (
        jax.ShapeDtypeStruct((ROWS, FEAT), BF16),
        jax.ShapeDtypeStruct((16, FEAT), F32),
    )
    made = pl.pallas_call(
        kernel,
        out_shape=results,
        in_specs=[anywhere] * 3,
        out_specs=(anywhere, pl.BlockSpec(memory_space=pltpu.VMEM)),
        scratch_shapes=[
            vm((FEAT, FEAT), BF16),
            vm((3, ROWS, FEAT), BF16),
            vm((ROWS, FEAT), BF16),
            vm((3, 2, ROWS, FEAT), BF16),
            vm((3, 2, ROWS, FEAT), BF16),
            vm((3, ROWS, FEAT), F32),
            vm((3, ROWS, 128), F32),
            vm((7, ROWS, ROWS), F32),
            vm((ROWS, 6 * ROWS), BF16),
            vm((3, ROWS, ROWS), BF16),
            vm((3, ROWS, 128), F32),
            vm((4, 3 * ROWS, 256), BF16),
            vm((2, 512, 3 * ROWS), BF16),
            vm((4, ROWS, 256), F32),
            vm((4, 2, 512, 128), BF16),
            vm((4, 2, 512, 128), BF16),
            vm((4, 4, 128, 128), BF16),
            vm((4, 4, 128, 128), BF16),
            vm((3, 4, 128, 128), BF16),
            vm((3, 4, 128, 128), BF16),
            vm((4, 128, 128), BF16),
            vm((4, 128, 128), BF16),
            vm((3, 128, 128), BF16),
            vm((3, 128, 128), BF16),
            vm((NZ, 16, 128), BF16),
            vm((NZ - 1, 16, 128), BF16),
            vm((NCLIP, 16, 128), F32),
            vm((2, 4, ROWS, 256), BF16),
            vm((ROWS, FEAT), BF16),
            vm((ROWS, FEAT), BF16),
            dma((3,)), dma((1,)),
            dma((2, 2 * PARTS)), dma((2, 2 * PARTS)),
            dma((4 + 2 * PARTS,)), dma((4 + 2 * PARTS,)),
            dma((2, 4)), dma((2, 4)),
            dma((4,)), dma((4,)),
            dma((3,)), dma((3,)),
            dma((3, 4)), dma((3, 4)),
            dma((2, 3)), dma((2, 3)),
            dma((NZ - 1,)), dma((NZ - 1,)),
            dma((NCLIP - 1,)), dma((NCLIP - 1,)),
            pltpu.SemaphoreType.REGULAR((WORDS, 6)),
        ],
        compiler_params=pltpu.CompilerParams(
            collective_id=0, has_side_effects=True, vmem_limit_bytes=56 * 2**20
        ),
    )(student_hidden[0], teacher_tokens[0], proj_weight)
    hidden_grad, weight_grad = pl.pallas_call(
        handed_on,
        out_shape=results,
        in_specs=[pl.BlockSpec(memory_space=pltpu.VMEM)] * 2,
        out_specs=(pl.BlockSpec(memory_space=pltpu.VMEM),) * 2,
    )(*made)
    return hidden_grad[None], weight_grad


def solution(mesh):
    placed = (P("clip", "tok", None), P("clip", "tok", None), P())
    return jax.shard_map(
        local,
        mesh=mesh,
        in_specs=placed,
        out_specs=(P("clip", "tok", None), P("tok", None)),
        check_vma=False,
    )
```

```python
import jax
import jax.numpy as jnp
from jax import lax
from jax.experimental import pallas as pl
from jax.experimental.pallas import tpu as pltpu
from jax.sharding import PartitionSpec as P

EPSILON = 1e-06
MESH = pl.DeviceIdType.MESH
BF16 = jnp.bfloat16
F32 = jnp.float32
ROWS = 256
FEAT = 1024
NZ, NY, NX, NCLIP = 16, 4, 4, 8
CHAINS = 32
PARTS = 2
PART = ROWS // PARTS
WORDS = 7
FAR = ((0, 0), (2, 0), (0, 1), (2, 1))
STEP = 32


def dot_nn(a, b):
    return jnp.dot(a, b, preferred_element_type=F32)


def dot_nt(a, b):
    return lax.dot_general(a, b, (((1,), (1,)), ((), ())), preferred_element_type=F32)


def kernel(
    h_ref, t_ref, w_ref, hg_ref, wg_ref,
    wv, hr, tr, su, tu, proj, inv, ds, e_near, e_far, acc, pall, ht,
    early, ws, wr, a0, a1, r0, r1, b0, b1, s0, s1, zs, zr, ag, pf, hgv, ov,
    load_sem, store_sem, halo_s, halo_r, fwd_s, fwd_r, pf_s, pf_r,
    d2d_s, d2d_r, st1_s, st1_r, st1b_s, st1b_r, st2_s, st2_r, z_s, z_r, ag_s, ag_r, word,
):
    k = lax.axis_index("clip")
    b = lax.axis_index("tok")
    c = lax.rem(b, 2)
    q = b // 2
    z = lax.rem(q, NZ)
    xl = q // NZ
    y = k // 2
    xh = lax.rem(k, 2)
    x = xh * 2 + xl
    has = (q > 0, q < CHAINS - 1)
    turn = (q == NZ, q == NZ - 1)
    corner = (2 * CHAINS - 2 + c, c)

    def at(yy, xx, zz, cc):
        return {"clip": yy * 2 + xx // 2, "tok": lax.rem(xx, 2) * 32 + zz * 2 + cc}

    sib = {"clip": k, "tok": b + 1 - 2 * c}
    side = ({"clip": k, "tok": b - 2}, {"clip": k, "tok": b + 2})

    def y_peer(d):
        return at(lax.rem(y + d, NY), x, z, c)

    def x_peer(d):
        return at(y, lax.rem(x + d, NX), z, c)

    def z_peer(d):
        return at(y, x, lax.rem(z + d, NZ), c)

    def remote(src, dst, ssem, rsem, dev):
        return pltpu.make_async_remote_copy(
            src_ref=src, dst_ref=dst, send_sem=ssem, recv_sem=rsem, device_id=dev, device_id_type=MESH
        )

    loads = [
        pltpu.make_async_copy(h_ref, hr.at[1], load_sem.at[0]),
        pltpu.make_async_copy(t_ref, tr, load_sem.at[1]),
        pltpu.make_async_copy(w_ref, wv, load_sem.at[2]),
    ]
    for cp in loads:
        cp.start()
    barrier = pltpu.get_barrier_semaphore()

    def greet(dev):
        pl.semaphore_signal(barrier, inc=1, device_id=dev, device_id_type=MESH)

    near_peers = (
        at(y, x, lax.rem(z + 1, NZ), c), at(y, x, lax.rem(z + NZ - 1, NZ), c),
        y_peer(1), y_peer(NY - 1), x_peer(1), x_peer(NX - 1),
    )
    for i in range(2):
        @pl.when(has[i])
        def _(i=i):
            greet(side[i])
    greet(sib)
    for dev in near_peers:
        greet(dev)
    ends = jnp.where(q > 0, 1, 0) + jnp.where(q < CHAINS - 1, 1, 0)

    def heard(n):
        for i in range(len(near_peers)):
            pl.semaphore_wait(word.at[n, i], 1)

    def pass_on(n):
        if n:
            heard(n - 1)
        for i, dev in enumerate(near_peers):
            pl.semaphore_signal(word.at[n, i], inc=1, device_id=dev, device_id_type=MESH)

    def teacher_unit():
        def body(i, carry):
            rows = pl.ds(pl.multiple_of(i * STEP, STEP), STEP)
            v = tr[rows].astype(F32)
            r = lax.rsqrt(jnp.sum(v * v, axis=-1, keepdims=True) + EPSILON)
            tu[1, 0, rows] = (v * r).astype(BF16)
            return carry

        lax.fori_loop(0, ROWS // STEP, body, 0)

    def student_unit(slot, first, n):
        rows_all = slice(first, first + n)

        def block(nb, carry):
            cols = pl.ds(pl.multiple_of(nb * 256, 256), 256)
            proj[slot, rows_all, cols] = dot_nn(hr[slot, rows_all], wv[:, cols])
            return carry

        lax.fori_loop(0, 4, block, 0)

        def body(i, carry):
            rows = pl.ds(pl.multiple_of(first + i * STEP, STEP), STEP)
            v = proj[slot, rows]
            r = lax.rsqrt(jnp.sum(v * v, axis=-1, keepdims=True) + EPSILON)
            inv[slot, rows] = jnp.broadcast_to(r, (STEP, 128))
            su[slot, 0, rows] = (v * r).astype(BF16)
            return carry

        lax.fori_loop(0, n // STEP, body, 0)

    def transposed(slot, n):
        for j in range(4):
            cols = slice(j * 256, (j + 1) * 256)
            v = hr[slot, n * PART : (n + 1) * PART, cols].astype(F32).T.reshape(8, 2, 16, PART)
            at_tokens = slice(slot * ROWS + n * PART, slot * ROWS + (n + 1) * PART)
            for cc in range(2):
                ht[cc, j * 128 : (j + 1) * 128, at_tokens] = v[:, cc].reshape(128, PART).astype(BF16)

    loads[0].wait()
    pl.semaphore_wait(barrier, 1 + len(near_peers) + ends)

    def part(n):
        return pl.ds(n * PART, PART)

    def halo_copy(i, n):
        slot = 2 - 2 * i
        sems = (halo_s.at[i, n], halo_r.at[i, n], side[i])
        if isinstance(n, int) and n < PARTS:
            return remote(hr.at[1, part(n)], hr.at[slot, part(n)], *sems)
        rows = pl.ds(pl.multiple_of((n - PARTS) * PART, PART), PART)
        return remote(tu.at[1, 0, rows], tu.at[slot, 0, rows], *sems)

    halo = [[halo_copy(i, n) for n in range(2 * PARTS)] for i in range(2)]

    def halo_send(n):
        for i in range(2):
            @pl.when(has[i])
            def _(i=i):
                halo[i][n].start()

    def halo_arrival(slot, n):
        i = slot // 2

        @pl.when(has[i])
        def _():
            halo[1 - i][n].wait_recv()

        @pl.when(jnp.logical_not(has[i]))
        def _():
            hr[slot, n * PART : (n + 1) * PART] = jnp.zeros((PART, FEAT), BF16)

    for n in range(PARTS):
        halo_send(n)
    pass_on(0)
    loads[1].wait()
    teacher_unit()
    for n in range(PARTS):
        halo_send(PARTS + n)
    loads[2].wait()
    student_unit(1, 0, ROWS)
    pass_on(1)

    fwd = []

    def forward(src, dst, n):
        cp = remote(src, dst, fwd_s.at[n], fwd_r.at[n], sib)
        cp.start()
        fwd.append(cp)
        return cp

    own_fwd = [
        forward(tu.at[1, 0], tu.at[1, 1], 0),
        forward(su.at[1, 0], su.at[1, 1], 1),
    ]
    for n in range(PARTS):
        transposed(1, n)
    for cp in own_fwd:
        cp.wait_recv()

    acc[...] = jnp.zeros_like(acc)

    def weigh(slot, student, teacher):
        w = (256.0 * (student - teacher)).astype(BF16)
        p = w.astype(F32) * student
        s = p[:, :128]
        if p.shape[1] == 256:
            s = s + p[:, 128:]
        acc[slot] = acc[slot] + s
        return w

    for who in range(2):
        e_near[:, who * 256 : (who + 1) * 256] = weigh(
            1, dot_nt(su[1, 0], su[1, who]), dot_nt(tu[1, 0], tu[1, who])
        )

    def own_gradient(nb, carry):
        cols = pl.ds(pl.multiple_of(nb * 256, 256), 256)
        early[nb] = dot_nn(e_near[:, 0:512], su[1, :, :, cols].reshape(512, 256))
        return carry

    lax.fori_loop(0, 4, own_gradient, 0)
    pass_on(2)

    s_fwd = []
    for n in range(PARTS):
        for slot in (0, 2):
            halo_arrival(slot, n)
            student_unit(slot, n * PART, PART)
            if n == PARTS - 1:
                s_fwd.append(forward(su.at[slot, 0], su.at[slot, 1], 2 + slot // 2))
            else:
                transposed(slot, n)
            pass_on(3 + n * 2 + slot // 2)
    for cp in s_fwd:
        cp.wait_recv()
    xs = 2 - 2 * c
    xo = 2 * c

    def far_pair(f):
        rows = jnp.where(f == 2, xs, 2 * f)
        return rows, 2 - rows, jnp.where(f == 2, 1, 0)

    def near_student(j, carry):
        ds[j] = dot_nt(su[1, 0], su[lax.rem(j, 2) * 2, j // 2])
        return carry

    lax.fori_loop(0, 4, near_student, 0)

    def far_student(f, carry):
        rows, slot, who = far_pair(f)
        ds[4 + f] = dot_nt(su[rows, 0], su[slot, who])
        return carry

    lax.fori_loop(0, 3, far_student, 0)

    def near_part(who, n):
        rows = pl.ds(pl.multiple_of(n * PART, PART), PART)
        cols = pl.ds(pl.multiple_of(512 + n * 4 * PART + who * 2 * PART, 2 * PART), 2 * PART)
        student = jnp.concatenate([ds[2 * who, :, rows], ds[2 * who + 1, :, rows]], axis=1)
        teacher = jnp.concatenate([tu[0, who, rows], tu[2, who, rows]], axis=0)
        e_near[:, cols] = weigh(1, student, dot_nt(tu[1, 0], teacher))

    def near_rows(n, cols):
        return jnp.concatenate([su[slot, who, n * PART : (n + 1) * PART, cols] for slot, who in FAR], axis=0)

    def teacher_part(n, carry):
        def arrived(slot):
            i = slot // 2
            rows = pl.ds(pl.multiple_of(n * PART, PART), PART)

            @pl.when(has[i])
            def _():
                halo_copy(1 - i, PARTS + n).wait_recv()

            @pl.when(jnp.logical_not(has[i]))
            def _():
                tu[slot, 0, rows] = jnp.zeros((PART, FEAT), BF16)

            cp = teacher_forward(slot, n)
            cp.start()
            return cp

        copies = [arrived(0), arrived(2)]

        near_part(0, n)

        @pl.when(n == PARTS - 1)
        def _():
            lax.fori_loop(0, 2, far_weight, 0)

        for cp in copies:
            cp.wait_recv()
        near_part(1, n)

        @pl.when(n == 0)
        def _():
            def block(nb, cc):
                cols = pl.ds(pl.multiple_of(nb * 256, 256), 256)
                early[nb] = early[nb] + dot_nn(e_near[:, 512:1024], near_rows(0, cols))
                return cc

            lax.fori_loop(0, 4, block, 0)
            for slot in (0, 2):
                transposed(slot, PARTS - 1)

        return carry

    def teacher_forward(slot, n):
        rows = pl.ds(pl.multiple_of(n * PART, PART), PART)
        m = 4 + n * 2 + slot // 2
        return remote(tu.at[slot, 0, rows], tu.at[slot, 1, rows], fwd_s.at[m], fwd_r.at[m], sib)

    def far_weight(f, carry):
        rows, slot, who = far_pair(f)
        e_far[f] = weigh(rows, ds[4 + f], dot_nt(tu[rows, 0], tu[slot, who]))
        return carry

    lax.fori_loop(0, PARTS, teacher_part, 0)
    far_weight(2, 0)
    for n in range(PARTS):
        for slot in (0, 2):
            fwd.append(teacher_forward(slot, n))

    def finish_along(i, carry):
        for slot in range(3):
            rows = pl.ds(pl.multiple_of(i * 64, 64), 64)
            along = jnp.sum(acc[slot, rows], axis=-1, keepdims=True)
            acc[slot, rows] = along * inv[slot, rows]
        return carry

    lax.fori_loop(0, ROWS // 64, finish_along, 0)

    heard(WORDS - 1)

    def offset(d):
        return jnp.where(d == 0, 2, jnp.where(d == 1, 1, jnp.where(d == 2, 3, 0)))

    def chunk(d):
        return lax.rem(y + offset(d), NY)

    def back_copy(i, d):
        yy = chunk(d)
        dev = {"clip": k, "tok": jnp.where(jnp.logical_and(turn[i], lax.rem(d, 2) == 1), corner[i], b + 4 * i - 2)}
        return remote(
            pall.at[yy, pl.ds(2 * i * ROWS, ROWS)], pf.at[1 - i, yy], pf_s.at[i, d], pf_r.at[i, d], dev
        )

    def relay_copy(i, d):
        yy = chunk(d)
        dev = {"clip": k, "tok": jnp.where(xl == 0, b + 32, b - 32)}
        return remote(pf.at[i, yy], pf.at[i, yy], pf_s.at[i, d], pf_r.at[1 - i, d], dev)

    def relay(d):
        for i in range(2):
            @pl.when(jnp.logical_not(has[i]))
            def _(i=i):
                relay_copy(i, d).wait_recv()
                relay_copy(i, d).start()

    def d2d_copy(d):
        return remote(ws.at[d], wr.at[d], d2d_s.at[d], d2d_r.at[d], sib)

    def first_y(d):
        return remote(a0.at[chunk(d)], r0.at[d], st1_s.at[d], st1_r.at[d], y_peer(offset(d)))

    def first_x(dx, d):
        yy = chunk(d)
        return remote(
            a1.at[lax.rem(x + dx, NX), yy], r1.at[dx - 1, yy], st1b_s.at[dx - 1, d], st1b_r.at[dx - 1, d], x_peer(dx)
        )

    def gradient(d):
        yy = chunk(d)
        cols = pl.ds(pl.multiple_of(yy * 256, 256), 256)
        grads = {
            1: early[yy] + dot_nn(e_near[:, 1024:1536], near_rows(1, cols)),
            0: dot_nn(e_far[0], su[2, 0, :, cols]),
            2: dot_nn(e_far[1], su[0, 0, :, cols]),
        }
        cross = dot_nn(e_far[2], su[xo, 1, :, cols])
        first = jnp.where(c == 1, 1.0, 0.0)
        grads[0] = grads[0] + first * cross
        grads[2] = grads[2] + (1.0 - first) * cross
        for slot in (0, 2, 1):
            for i in range(2):
                at_cols = pl.ds(pl.multiple_of(yy * 256 + i * 128, 128), 128)
                v = grads[slot][:, i * 128 : (i + 1) * 128]
                v = (v - proj[slot, :, at_cols] * acc[slot]) * inv[slot]
                pall[yy, slot * ROWS : (slot + 1) * ROWS, i * 128 : (i + 1) * 128] = v.astype(BF16)
        for i in range(2):
            @pl.when(has[i])
            def _(i=i):
                back_copy(i, d).start()

    def weight_sibling(d):
        part_sib = dot_nn(ht[1 - c], pall[chunk(d)])
        for i in range(2):
            ws[d, i] = part_sib[:, i * 128 : (i + 1) * 128].astype(BF16)
        d2d_copy(d).start()

    def reduce_first(d):
        yy = chunk(d)
        part_own = dot_nn(ht[c], pall[yy])
        d2d_copy(d).wait_recv()
        for i in range(2):
            v = (part_own[:, i * 128 : (i + 1) * 128] + wr[d, i].astype(F32)).astype(BF16)
            for j in range(2):
                a0[yy, i * 2 + j] = v[j * 256 : j * 256 + 128]
                a1[i * 2 + j, yy] = v[j * 256 + 128 : j * 256 + 256]

        @pl.when(d < 3)
        def _():
            first_y(d).start()

        for dx in (2, 1, 3):
            first_x(dx, d).start()

    def step(s, carry):
        @pl.when(s < 4)
        def _():
            gradient(s)
            weight_sibling(s)

        @pl.when(s > 0)
        def _():
            reduce_first(s - 1)

        return carry

    lax.fori_loop(0, 5, step, 0)
    back = [[back_copy(i, d) for d in range(4)] for i in range(2)]
    d2d = [d2d_copy(d) for d in range(4)]
    st1 = [first_y(d) for d in range(3)]
    st1b = [first_x(dx, d) for dx in (1, 2, 3) for d in range(4)]

    relay(1)
    st2 = []
    for cp in st1:
        cp.wait_recv()
    for dx in (2, 1, 3, 0):
        xx = lax.rem(x + dx, NX)
        v = a0[y, xx].astype(F32)
        for i in range(3):
            v = v + r0[i, xx].astype(F32)
        b0[xx] = v.astype(BF16)
        if dx:
            cp = remote(b0.at[xx], s0.at[dx - 1], st2_s.at[0, dx - 1], st2_r.at[0, dx - 1], x_peer(dx))
            cp.start()
            st2.append(cp)
    for cp in st1b:
        cp.wait_recv()
    relay(3)
    for dy in (2, 1, 3, 0):
        yy = lax.rem(y + dy, NY)
        v = a1[x, yy].astype(F32)
        for i in range(3):
            v = v + r1[i, yy].astype(F32)
        b1[yy] = v.astype(BF16)
        if dy:
            cp = remote(b1.at[yy], s1.at[dy - 1], st2_s.at[1, dy - 1], st2_r.at[1, dy - 1], y_peer(dy))
            cp.start()
            st2.append(cp)
    for cp in st2:
        cp.wait_recv()
    for half, own, got in ((0, b0[x], s0), (1, b1[y], s1)):
        v = own.astype(F32)
        for i in range(3):
            v = v + got[i].astype(F32)
        zs[half * 8 : half * 8 + 8] = v.reshape(8, 16, 128).astype(BF16)
    zc = []
    for d in (8, 7, 9, 6, 10, 5, 11, 4, 12, 3, 13, 2, 14, 1, 15):
        cp = remote(zs.at[lax.rem(z + d, NZ)], zr.at[d - 1], z_s.at[d - 1], z_r.at[d - 1], z_peer(d))
        cp.start()
        zc.append(cp)

    def hidden_gradient():
        for i in range(2):
            @pl.when(has[i])
            def _(i=i):
                for d in range(4):
                    back[1 - i][d].wait_recv()

            @pl.when(jnp.logical_not(has[i]))
            def _(i=i):
                for d in (1, 3):
                    relay_copy(i, d).wait_send()
                pf[i] = jnp.zeros((4, ROWS, 256), BF16)

        for nb in range(4):
            v = pall[nb, ROWS : 2 * ROWS].astype(F32) + pf[0, nb].astype(F32) + pf[1, nb].astype(F32)
            hgv[:, nb * 256 : (nb + 1) * 256] = v.astype(BF16)

        def block(nb, carry):
            at_block = pl.ds(pl.multiple_of(nb * 256, 256), 256)
            ov[:, at_block] = dot_nt(hgv[...], wv[at_block]).astype(BF16)
            return carry

        lax.fori_loop(0, 4, block, 0)

    def weight_gather():
        v = zs[z].astype(F32)
        for cp in zc:
            cp.wait_recv()
        for d in range(NZ - 1):
            v = v + zr[d].astype(F32)
        ag[k] = v * (1.0 / 1024.0)
        copies = []
        for n, (dy, dh) in enumerate(((2, 1), (1, 1), (3, 1), (2, 0), (0, 1), (1, 0), (3, 0))):
            dev = {"clip": lax.rem(y + dy, NY) * 2 + (1 - xh if dh else xh), "tok": b}
            cp = remote(ag.at[k], ag.at[k], ag_s.at[n], ag_r.at[n], dev)
            cp.start()
            copies.append(cp)
        return copies

    agc = weight_gather()
    hidden_gradient()
    store = pltpu.make_async_copy(ov, hg_ref, store_sem.at[0])
    store.start()
    for cp in agc:
        cp.wait_recv()
    for i in range(NCLIP):
        wg_ref[:, i * 128 : (i + 1) * 128] = ag[i]

    for i in range(2):
        @pl.when(has[i])
        def _(i=i):
            for cp in halo[i] + back[i]:
                cp.wait_send()
    for cp in fwd + d2d + st1 + st1b + st2 + zc + agc:
        cp.wait_send()
    store.wait()


def handed_on(hg_in, wg_in, hg_out, wg_out):
    hg_out[...] = hg_in[...]
    wg_out[...] = wg_in[...]


def local(student_hidden, teacher_tokens, proj_weight):
    dma = pltpu.SemaphoreType.DMA
    vm = pltpu.VMEM
    anywhere = pl.BlockSpec(memory_space=pl.ANY)
    results = (
        jax.ShapeDtypeStruct((ROWS, FEAT), BF16),
        jax.ShapeDtypeStruct((16, FEAT), F32),
    )
    made = pl.pallas_call(
        kernel,
        out_shape=results,
        in_specs=[anywhere] * 3,
        out_specs=(anywhere, pl.BlockSpec(memory_space=pltpu.VMEM)),
        scratch_shapes=[
            vm((FEAT, FEAT), BF16),
            vm((3, ROWS, FEAT), BF16),
            vm((ROWS, FEAT), BF16),
            vm((3, 2, ROWS, FEAT), BF16),
            vm((3, 2, ROWS, FEAT), BF16),
            vm((3, ROWS, FEAT), F32),
            vm((3, ROWS, 128), F32),
            vm((7, ROWS, ROWS), F32),
            vm((ROWS, 6 * ROWS), BF16),
            vm((3, ROWS, ROWS), BF16),
            vm((3, ROWS, 128), F32),
            vm((4, 3 * ROWS, 256), BF16),
            vm((2, 512, 3 * ROWS), BF16),
            vm((4, ROWS, 256), F32),
            vm((4, 2, 512, 128), BF16),
            vm((4, 2, 512, 128), BF16),
            vm((4, 4, 128, 128), BF16),
            vm((4, 4, 128, 128), BF16),
            vm((3, 4, 128, 128), BF16),
            vm((3, 4, 128, 128), BF16),
            vm((4, 128, 128), BF16),
            vm((4, 128, 128), BF16),
            vm((3, 128, 128), BF16),
            vm((3, 128, 128), BF16),
            vm((NZ, 16, 128), BF16),
            vm((NZ - 1, 16, 128), BF16),
            vm((NCLIP, 16, 128), F32),
            vm((2, 4, ROWS, 256), BF16),
            vm((ROWS, FEAT), BF16),
            vm((ROWS, FEAT), BF16),
            dma((3,)), dma((1,)),
            dma((2, 2 * PARTS)), dma((2, 2 * PARTS)),
            dma((4 + 2 * PARTS,)), dma((4 + 2 * PARTS,)),
            dma((2, 4)), dma((2, 4)),
            dma((4,)), dma((4,)),
            dma((3,)), dma((3,)),
            dma((3, 4)), dma((3, 4)),
            dma((2, 3)), dma((2, 3)),
            dma((NZ - 1,)), dma((NZ - 1,)),
            dma((NCLIP - 1,)), dma((NCLIP - 1,)),
            pltpu.SemaphoreType.REGULAR((WORDS, 6)),
        ],
        compiler_params=pltpu.CompilerParams(
            collective_id=0, has_side_effects=True, vmem_limit_bytes=56 * 2**20
        ),
    )(student_hidden[0], teacher_tokens[0], proj_weight)
    hidden_grad, weight_grad = pl.pallas_call(
        handed_on,
        out_shape=results,
        in_specs=[pl.BlockSpec(memory_space=pltpu.VMEM)] * 2,
        out_specs=(pl.BlockSpec(memory_space=pltpu.VMEM),) * 2,
    )(*made)
    return hidden_grad[None], weight_grad


def solution(mesh):
    placed = (P("clip", "tok", None), P("clip", "tok", None), P())
    return jax.shard_map(
        local,
        mesh=mesh,
        in_specs=placed,
        out_specs=(P("clip", "tok", None), P("tok", None)),
        check_vma=False,
    )
```

```python
import jax
import jax.numpy as jnp
from jax import lax
from jax.experimental import pallas as pl
from jax.experimental.pallas import tpu as pltpu
from jax.sharding import PartitionSpec as P

EPSILON = 1e-06
MESH = pl.DeviceIdType.MESH
BF16 = jnp.bfloat16
F32 = jnp.float32
ROWS = 256
FEAT = 1024
NZ, NY, NX, NCLIP = 16, 4, 4, 8
CHAINS = 32
PARTS = 2
PART = ROWS // PARTS
WORDS = 7
SUB = 64
SUBS = ROWS // SUB
FAR = ((0, 0), (2, 0), (0, 1), (2, 1))
STEP = 32


def dot_nn(a, b):
    return jnp.dot(a, b, preferred_element_type=F32)


def dot_nt(a, b):
    return lax.dot_general(a, b, (((1,), (1,)), ((), ())), preferred_element_type=F32)


def kernel(
    h_ref, t_ref, w_ref, hg_ref, wg_ref,
    wv, hr, tr, su, tu, proj, inv, ds, e_near, e_far, acc, pall, ht,
    early, ws, wr, a0, a1, r0, r1, b0, b1, s0, s1, zs, zr, ag, pf, hgv, ov,
    load_sem, store_sem, halo_s, halo_r, fwd_s, fwd_r, pf_s, pf_r,
    d2d_s, d2d_r, st1_s, st1_r, st1b_s, st1b_r, st2_s, st2_r, z_s, z_r, ag_s, ag_r, word,
):
    k = lax.axis_index("clip")
    b = lax.axis_index("tok")
    c = lax.rem(b, 2)
    q = b // 2
    z = lax.rem(q, NZ)
    xl = q // NZ
    y = k // 2
    xh = lax.rem(k, 2)
    x = xh * 2 + xl
    has = (q > 0, q < CHAINS - 1)
    turn = (q == NZ, q == NZ - 1)
    corner = (2 * CHAINS - 2 + c, c)

    def at(yy, xx, zz, cc):
        return {"clip": yy * 2 + xx // 2, "tok": lax.rem(xx, 2) * 32 + zz * 2 + cc}

    sib = {"clip": k, "tok": b + 1 - 2 * c}
    side = ({"clip": k, "tok": b - 2}, {"clip": k, "tok": b + 2})

    def y_peer(d):
        return at(lax.rem(y + d, NY), x, z, c)

    def x_peer(d):
        return at(y, lax.rem(x + d, NX), z, c)

    def z_peer(d):
        return at(y, x, lax.rem(z + d, NZ), c)

    def remote(src, dst, ssem, rsem, dev):
        return pltpu.make_async_remote_copy(
            src_ref=src, dst_ref=dst, send_sem=ssem, recv_sem=rsem, device_id=dev, device_id_type=MESH
        )

    loads = [
        pltpu.make_async_copy(h_ref, hr.at[1], load_sem.at[0]),
        pltpu.make_async_copy(t_ref, tr, load_sem.at[1]),
        pltpu.make_async_copy(w_ref, wv, load_sem.at[2]),
    ]
    for cp in loads:
        cp.start()
    barrier = pltpu.get_barrier_semaphore()

    def greet(dev):
        pl.semaphore_signal(barrier, inc=1, device_id=dev, device_id_type=MESH)

    near_peers = (
        at(y, x, lax.rem(z + 1, NZ), c), at(y, x, lax.rem(z + NZ - 1, NZ), c),
        y_peer(1), y_peer(NY - 1), x_peer(1), x_peer(NX - 1),
    )
    for i in range(2):
        @pl.when(has[i])
        def _(i=i):
            greet(side[i])
    greet(sib)
    for dev in near_peers:
        greet(dev)
    ends = jnp.where(q > 0, 1, 0) + jnp.where(q < CHAINS - 1, 1, 0)

    def heard(n):
        for i in range(len(near_peers)):
            pl.semaphore_wait(word.at[n, i], 1)

    def pass_on(n):
        if n:
            heard(n - 1)
        for i, dev in enumerate(near_peers):
            pl.semaphore_signal(word.at[n, i], inc=1, device_id=dev, device_id_type=MESH)

    def teacher_unit():
        def body(i, carry):
            rows = pl.ds(pl.multiple_of(i * STEP, STEP), STEP)
            v = tr[rows].astype(F32)
            r = lax.rsqrt(jnp.sum(v * v, axis=-1, keepdims=True) + EPSILON)
            tu[1, 0, rows] = (v * r).astype(BF16)
            return carry

        lax.fori_loop(0, ROWS // STEP, body, 0)

    def student_unit(slot, first, n):
        rows_all = slice(first, first + n)

        def block(nb, carry):
            cols = pl.ds(pl.multiple_of(nb * 256, 256), 256)
            proj[slot, rows_all, cols] = dot_nn(hr[slot, rows_all], wv[:, cols])
            return carry

        lax.fori_loop(0, 4, block, 0)

        def body(i, carry):
            rows = pl.ds(pl.multiple_of(first + i * STEP, STEP), STEP)
            v = proj[slot, rows]
            r = lax.rsqrt(jnp.sum(v * v, axis=-1, keepdims=True) + EPSILON)
            inv[slot, rows] = jnp.broadcast_to(r, (STEP, 128))
            su[slot, 0, rows] = (v * r).astype(BF16)
            return carry

        lax.fori_loop(0, n // STEP, body, 0)

    def transposed(slot, n):
        for j in range(4):
            cols = slice(j * 256, (j + 1) * 256)
            v = hr[slot, n * PART : (n + 1) * PART, cols].astype(F32).T.reshape(8, 2, 16, PART)
            at_tokens = slice(slot * ROWS + n * PART, slot * ROWS + (n + 1) * PART)
            for cc in range(2):
                ht[cc, j * 128 : (j + 1) * 128, at_tokens] = v[:, cc].reshape(128, PART).astype(BF16)

    loads[0].wait()
    pl.semaphore_wait(barrier, 1 + len(near_peers) + ends)

    def part(n):
        return pl.ds(n * PART, PART)

    def halo_copy(i, n):
        slot = 2 - 2 * i
        sems = (halo_s.at[i, n], halo_r.at[i, n], side[i])
        if isinstance(n, int) and n < PARTS:
            return remote(hr.at[1, part(n)], hr.at[slot, part(n)], *sems)
        rows = pl.ds(pl.multiple_of((n - PARTS) * SUB, SUB), SUB)
        return remote(tu.at[1, 0, rows], tu.at[slot, 0, rows], *sems)

    halo = [[halo_copy(i, n) for n in range(PARTS + SUBS)] for i in range(2)]

    def halo_send(n):
        for i in range(2):
            @pl.when(has[i])
            def _(i=i):
                halo[i][n].start()

    def halo_arrival(slot, n):
        i = slot // 2

        @pl.when(has[i])
        def _():
            halo[1 - i][n].wait_recv()

        @pl.when(jnp.logical_not(has[i]))
        def _():
            hr[slot, n * PART : (n + 1) * PART] = jnp.zeros((PART, FEAT), BF16)

    for n in range(PARTS):
        halo_send(n)
    pass_on(0)
    loads[1].wait()
    teacher_unit()
    for n in range(SUBS):
        halo_send(PARTS + n)
    loads[2].wait()
    student_unit(1, 0, ROWS)
    pass_on(1)

    fwd = []

    def forward(src, dst, n):
        cp = remote(src, dst, fwd_s.at[n], fwd_r.at[n], sib)
        cp.start()
        fwd.append(cp)
        return cp

    own_fwd = [
        forward(tu.at[1, 0], tu.at[1, 1], 0),
        forward(su.at[1, 0], su.at[1, 1], 1),
    ]
    for n in range(PARTS):
        transposed(1, n)
    for cp in own_fwd:
        cp.wait_recv()

    acc[...] = jnp.zeros_like(acc)

    def weigh(slot, student, teacher):
        w = (256.0 * (student - teacher)).astype(BF16)
        p = w.astype(F32) * student
        s = p[:, :128]
        if p.shape[1] == 256:
            s = s + p[:, 128:]
        acc[slot] = acc[slot] + s
        return w

    for who in range(2):
        e_near[:, who * 256 : (who + 1) * 256] = weigh(
            1, dot_nt(su[1, 0], su[1, who]), dot_nt(tu[1, 0], tu[1, who])
        )

    def own_gradient(nb, carry):
        cols = pl.ds(pl.multiple_of(nb * 256, 256), 256)
        early[nb] = dot_nn(e_near[:, 0:512], su[1, :, :, cols].reshape(512, 256))
        return carry

    lax.fori_loop(0, 4, own_gradient, 0)
    pass_on(2)

    s_fwd = []
    for n in range(PARTS):
        for slot in (0, 2):
            halo_arrival(slot, n)
            student_unit(slot, n * PART, PART)
            if n == PARTS - 1:
                s_fwd.append(forward(su.at[slot, 0], su.at[slot, 1], 2 + slot // 2))
            else:
                transposed(slot, n)
            pass_on(3 + n * 2 + slot // 2)
    for cp in s_fwd:
        cp.wait_recv()
    xs = 2 - 2 * c
    xo = 2 * c

    def far_pair(f):
        rows = jnp.where(f == 2, xs, 2 * f)
        return rows, 2 - rows, jnp.where(f == 2, 1, 0)

    def near_student(j, carry):
        ds[j] = dot_nt(su[1, 0], su[lax.rem(j, 2) * 2, j // 2])
        return carry

    lax.fori_loop(0, 4, near_student, 0)

    def far_student(f, carry):
        rows, slot, who = far_pair(f)
        ds[4 + f] = dot_nt(su[rows, 0], su[slot, who])
        return carry

    lax.fori_loop(0, 3, far_student, 0)

    def near_part(who, n):
        rows = pl.ds(pl.multiple_of(n * PART, PART), PART)
        cols = pl.ds(pl.multiple_of(512 + n * 4 * PART + who * 2 * PART, 2 * PART), 2 * PART)
        student = jnp.concatenate([ds[2 * who, :, rows], ds[2 * who + 1, :, rows]], axis=1)
        teacher = jnp.concatenate([tu[0, who, rows], tu[2, who, rows]], axis=0)
        e_near[:, cols] = weigh(1, student, dot_nt(tu[1, 0], teacher))

    def near_rows(n, cols):
        return jnp.concatenate([su[slot, who, n * PART : (n + 1) * PART, cols] for slot, who in FAR], axis=0)

    def teacher_part(n, carry):
        def arrived(slot, m):
            i = slot // 2
            rows = pl.ds(pl.multiple_of(m * SUB, SUB), SUB)

            @pl.when(has[i])
            def _():
                halo_copy(1 - i, PARTS + m).wait_recv()

            @pl.when(jnp.logical_not(has[i]))
            def _():
                tu[slot, 0, rows] = jnp.zeros((SUB, FEAT), BF16)

            cp = teacher_forward(slot, m)
            cp.start()
            return cp

        copies = [arrived(slot, n * (SUBS // PARTS) + m) for m in range(SUBS // PARTS) for slot in (0, 2)]

        near_part(0, n)

        @pl.when(n == PARTS - 1)
        def _():
            lax.fori_loop(0, 2, far_weight, 0)

        for cp in copies:
            cp.wait_recv()
        near_part(1, n)

        @pl.when(n == 0)
        def _():
            def block(nb, cc):
                cols = pl.ds(pl.multiple_of(nb * 256, 256), 256)
                early[nb] = early[nb] + dot_nn(e_near[:, 512:1024], near_rows(0, cols))
                return cc

            lax.fori_loop(0, 4, block, 0)
            for slot in (0, 2):
                transposed(slot, PARTS - 1)

        return carry

    def teacher_forward(slot, n):
        rows = pl.ds(pl.multiple_of(n * SUB, SUB), SUB)
        m = 4 + n * 2 + slot // 2
        return remote(tu.at[slot, 0, rows], tu.at[slot, 1, rows], fwd_s.at[m], fwd_r.at[m], sib)

    def far_weight(f, carry):
        rows, slot, who = far_pair(f)
        e_far[f] = weigh(rows, ds[4 + f], dot_nt(tu[rows, 0], tu[slot, who]))
        return carry

    lax.fori_loop(0, PARTS, teacher_part, 0)
    far_weight(2, 0)
    for n in range(SUBS):
        for slot in (0, 2):
            fwd.append(teacher_forward(slot, n))

    def finish_along(i, carry):
        for slot in range(3):
            rows = pl.ds(pl.multiple_of(i * 64, 64), 64)
            along = jnp.sum(acc[slot, rows], axis=-1, keepdims=True)
            acc[slot, rows] = along * inv[slot, rows]
        return carry

    lax.fori_loop(0, ROWS // 64, finish_along, 0)

    heard(WORDS - 1)

    def offset(d):
        return jnp.where(d == 0, 2, jnp.where(d == 1, 1, jnp.where(d == 2, 3, 0)))

    def chunk(d):
        return lax.rem(y + offset(d), NY)

    def back_copy(i, d):
        yy = chunk(d)
        dev = {"clip": k, "tok": jnp.where(jnp.logical_and(turn[i], lax.rem(d, 2) == 1), corner[i], b + 4 * i - 2)}
        return remote(
            pall.at[yy, pl.ds(2 * i * ROWS, ROWS)], pf.at[1 - i, yy], pf_s.at[i, d], pf_r.at[i, d], dev
        )

    def relay_copy(i, d):
        yy = chunk(d)
        dev = {"clip": k, "tok": jnp.where(xl == 0, b + 32, b - 32)}
        return remote(pf.at[i, yy], pf.at[i, yy], pf_s.at[i, d], pf_r.at[1 - i, d], dev)

    def relay(d):
        for i in range(2):
            @pl.when(jnp.logical_not(has[i]))
            def _(i=i):
                relay_copy(i, d).wait_recv()
                relay_copy(i, d).start()

    def d2d_copy(d):
        return remote(ws.at[d], wr.at[d], d2d_s.at[d], d2d_r.at[d], sib)

    def first_y(d):
        return remote(a0.at[chunk(d)], r0.at[d], st1_s.at[d], st1_r.at[d], y_peer(offset(d)))

    def first_x(dx, d):
        yy = chunk(d)
        return remote(
            a1.at[lax.rem(x + dx, NX), yy], r1.at[dx - 1, yy], st1b_s.at[dx - 1, d], st1b_r.at[dx - 1, d], x_peer(dx)
        )

    def gradient(d):
        yy = chunk(d)
        cols = pl.ds(pl.multiple_of(yy * 256, 256), 256)
        grads = {
            1: early[yy] + dot_nn(e_near[:, 1024:1536], near_rows(1, cols)),
            0: dot_nn(e_far[0], su[2, 0, :, cols]),
            2: dot_nn(e_far[1], su[0, 0, :, cols]),
        }
        cross = dot_nn(e_far[2], su[xo, 1, :, cols])
        first = jnp.where(c == 1, 1.0, 0.0)
        grads[0] = grads[0] + first * cross
        grads[2] = grads[2] + (1.0 - first) * cross
        for slot in (0, 2, 1):
            for i in range(2):
                at_cols = pl.ds(pl.multiple_of(yy * 256 + i * 128, 128), 128)
                v = grads[slot][:, i * 128 : (i + 1) * 128]
                v = (v - proj[slot, :, at_cols] * acc[slot]) * inv[slot]
                pall[yy, slot * ROWS : (slot + 1) * ROWS, i * 128 : (i + 1) * 128] = v.astype(BF16)
        for i in range(2):
            @pl.when(has[i])
            def _(i=i):
                back_copy(i, d).start()

    def weight_sibling(d):
        part_sib = dot_nn(ht[1 - c], pall[chunk(d)])
        for i in range(2):
            ws[d, i] = part_sib[:, i * 128 : (i + 1) * 128].astype(BF16)
        d2d_copy(d).start()

    def reduce_first(d):
        yy = chunk(d)
        part_own = dot_nn(ht[c], pall[yy])
        d2d_copy(d).wait_recv()
        for i in range(2):
            v = (part_own[:, i * 128 : (i + 1) * 128] + wr[d, i].astype(F32)).astype(BF16)
            for j in range(2):
                a0[yy, i * 2 + j] = v[j * 256 : j * 256 + 128]
                a1[i * 2 + j, yy] = v[j * 256 + 128 : j * 256 + 256]

        @pl.when(d < 3)
        def _():
            first_y(d).start()

        for dx in (2, 1, 3):
            first_x(dx, d).start()

    def step(s, carry):
        @pl.when(s < 4)
        def _():
            gradient(s)
            weight_sibling(s)

        @pl.when(s > 0)
        def _():
            reduce_first(s - 1)

        return carry

    lax.fori_loop(0, 5, step, 0)
    back = [[back_copy(i, d) for d in range(4)] for i in range(2)]
    d2d = [d2d_copy(d) for d in range(4)]
    st1 = [first_y(d) for d in range(3)]
    st1b = [first_x(dx, d) for dx in (1, 2, 3) for d in range(4)]

    relay(1)
    st2 = []
    for cp in st1:
        cp.wait_recv()
    for dx in (2, 1, 3, 0):
        xx = lax.rem(x + dx, NX)
        v = a0[y, xx].astype(F32)
        for i in range(3):
            v = v + r0[i, xx].astype(F32)
        b0[xx] = v.astype(BF16)
        if dx:
            cp = remote(b0.at[xx], s0.at[dx - 1], st2_s.at[0, dx - 1], st2_r.at[0, dx - 1], x_peer(dx))
            cp.start()
            st2.append(cp)
    for cp in st1b:
        cp.wait_recv()
    relay(3)
    for dy in (2, 1, 3, 0):
        yy = lax.rem(y + dy, NY)
        v = a1[x, yy].astype(F32)
        for i in range(3):
            v = v + r1[i, yy].astype(F32)
        b1[yy] = v.astype(BF16)
        if dy:
            cp = remote(b1.at[yy], s1.at[dy - 1], st2_s.at[1, dy - 1], st2_r.at[1, dy - 1], y_peer(dy))
            cp.start()
            st2.append(cp)
    for cp in st2:
        cp.wait_recv()
    for half, own, got in ((0, b0[x], s0), (1, b1[y], s1)):
        v = own.astype(F32)
        for i in range(3):
            v = v + got[i].astype(F32)
        zs[half * 8 : half * 8 + 8] = v.reshape(8, 16, 128).astype(BF16)
    zc = []
    for d in (8, 7, 9, 6, 10, 5, 11, 4, 12, 3, 13, 2, 14, 1, 15):
        cp = remote(zs.at[lax.rem(z + d, NZ)], zr.at[d - 1], z_s.at[d - 1], z_r.at[d - 1], z_peer(d))
        cp.start()
        zc.append(cp)

    def hidden_gradient():
        for i in range(2):
            @pl.when(has[i])
            def _(i=i):
                for d in range(4):
                    back[1 - i][d].wait_recv()

            @pl.when(jnp.logical_not(has[i]))
            def _(i=i):
                for d in (1, 3):
                    relay_copy(i, d).wait_send()
                pf[i] = jnp.zeros((4, ROWS, 256), BF16)

        for nb in range(4):
            v = pall[nb, ROWS : 2 * ROWS].astype(F32) + pf[0, nb].astype(F32) + pf[1, nb].astype(F32)
            hgv[:, nb * 256 : (nb + 1) * 256] = v.astype(BF16)

        def block(nb, carry):
            at_block = pl.ds(pl.multiple_of(nb * 256, 256), 256)
            ov[:, at_block] = dot_nt(hgv[...], wv[at_block]).astype(BF16)
            return carry

        lax.fori_loop(0, 4, block, 0)

    def weight_gather():
        v = zs[z].astype(F32)
        for cp in zc:
            cp.wait_recv()
        for d in range(NZ - 1):
            v = v + zr[d].astype(F32)
        ag[k] = v * (1.0 / 1024.0)
        copies = []
        for n, (dy, dh) in enumerate(((2, 1), (1, 1), (3, 1), (2, 0), (0, 1), (1, 0), (3, 0))):
            dev = {"clip": lax.rem(y + dy, NY) * 2 + (1 - xh if dh else xh), "tok": b}
            cp = remote(ag.at[k], ag.at[k], ag_s.at[n], ag_r.at[n], dev)
            cp.start()
            copies.append(cp)
        return copies

    agc = weight_gather()
    hidden_gradient()
    store = pltpu.make_async_copy(ov, hg_ref, store_sem.at[0])
    store.start()
    for cp in agc:
        cp.wait_recv()
    for i in range(NCLIP):
        wg_ref[:, i * 128 : (i + 1) * 128] = ag[i]

    for i in range(2):
        @pl.when(has[i])
        def _(i=i):
            for cp in halo[i] + back[i]:
                cp.wait_send()
    for cp in fwd + d2d + st1 + st1b + st2 + zc + agc:
        cp.wait_send()
    store.wait()


def handed_on(hg_in, wg_in, hg_out, wg_out):
    hg_out[...] = hg_in[...]
    wg_out[...] = wg_in[...]


def local(student_hidden, teacher_tokens, proj_weight):
    dma = pltpu.SemaphoreType.DMA
    vm = pltpu.VMEM
    anywhere = pl.BlockSpec(memory_space=pl.ANY)
    results = (
        jax.ShapeDtypeStruct((ROWS, FEAT), BF16),
        jax.ShapeDtypeStruct((16, FEAT), F32),
    )
    made = pl.pallas_call(
        kernel,
        out_shape=results,
        in_specs=[anywhere] * 3,
        out_specs=(anywhere, pl.BlockSpec(memory_space=pltpu.VMEM)),
        scratch_shapes=[
            vm((FEAT, FEAT), BF16),
            vm((3, ROWS, FEAT), BF16),
            vm((ROWS, FEAT), BF16),
            vm((3, 2, ROWS, FEAT), BF16),
            vm((3, 2, ROWS, FEAT), BF16),
            vm((3, ROWS, FEAT), F32),
            vm((3, ROWS, 128), F32),
            vm((7, ROWS, ROWS), F32),
            vm((ROWS, 6 * ROWS), BF16),
            vm((3, ROWS, ROWS), BF16),
            vm((3, ROWS, 128), F32),
            vm((4, 3 * ROWS, 256), BF16),
            vm((2, 512, 3 * ROWS), BF16),
            vm((4, ROWS, 256), F32),
            vm((4, 2, 512, 128), BF16),
            vm((4, 2, 512, 128), BF16),
            vm((4, 4, 128, 128), BF16),
            vm((4, 4, 128, 128), BF16),
            vm((3, 4, 128, 128), BF16),
            vm((3, 4, 128, 128), BF16),
            vm((4, 128, 128), BF16),
            vm((4, 128, 128), BF16),
            vm((3, 128, 128), BF16),
            vm((3, 128, 128), BF16),
            vm((NZ, 16, 128), BF16),
            vm((NZ - 1, 16, 128), BF16),
            vm((NCLIP, 16, 128), F32),
            vm((2, 4, ROWS, 256), BF16),
            vm((ROWS, FEAT), BF16),
            vm((ROWS, FEAT), BF16),
            dma((3,)), dma((1,)),
            dma((2, PARTS + SUBS)), dma((2, PARTS + SUBS)),
            dma((4 + 2 * SUBS,)), dma((4 + 2 * SUBS,)),
            dma((2, 4)), dma((2, 4)),
            dma((4,)), dma((4,)),
            dma((3,)), dma((3,)),
            dma((3, 4)), dma((3, 4)),
            dma((2, 3)), dma((2, 3)),
            dma((NZ - 1,)), dma((NZ - 1,)),
            dma((NCLIP - 1,)), dma((NCLIP - 1,)),
            pltpu.SemaphoreType.REGULAR((WORDS, 6)),
        ],
        compiler_params=pltpu.CompilerParams(
            collective_id=0, has_side_effects=True, vmem_limit_bytes=56 * 2**20
        ),
    )(student_hidden[0], teacher_tokens[0], proj_weight)
    hidden_grad, weight_grad = pl.pallas_call(
        handed_on,
        out_shape=results,
        in_specs=[pl.BlockSpec(memory_space=pltpu.VMEM)] * 2,
        out_specs=(pl.BlockSpec(memory_space=pltpu.VMEM),) * 2,
    )(*made)
    return hidden_grad[None], weight_grad


def solution(mesh):
    placed = (P("clip", "tok", None), P("clip", "tok", None), P())
    return jax.shard_map(
        local,
        mesh=mesh,
        in_specs=placed,
        out_specs=(P("clip", "tok", None), P("tok", None)),
        check_vma=False,
    )
```
